32 devices in a mesh: ctx: 8 (over y, x, core), tp: 4 (over z).
Axes of the slice: x: 2, y: 2, z: 4, core: 2. Of those that a mesh axis runs over, the one named last changes fastest.
Arguments:
- queries: bfloat16 [2048, 2048], P('ctx', 'tp'), may hold values from -24 to 24
- key_heads: bfloat16 [2048, 4, 128], P('ctx'), may hold values from -6 to 6
- head_values: bfloat16 [2048, 4, 128], P('ctx'), may hold values from -6 to 6
- hidden: bfloat16 [2048, 4096], P('ctx'), may hold values from -0.59765625 to 0.59765625
- out_proj: bfloat16 [2048, 4096], P('tp'), may hold values from -0.125 to 0.125
- norm_gain: float32 [4096], replicated, may hold values from 0.25 to 1.75
- x_proj: bfloat16 [4096, 4096], P('ctx', 'tp'), may hold values from -0.046875 to 0.046875
- bc_proj: bfloat16 [4096, 4, 256], P('ctx'), may hold values from -0.09375 to 0.09375
- dt_proj: bfloat16 [4096, 64], P('ctx', 'tp'), may hold values from -0.09375 to 0.09375
- dt_bias: float32 [64], P('tp'), may hold values from -12 to 0
- decay_log: float32 [64], P('tp'), may hold values from -10 to 3
- skip_gain: float32 [64], P('tp'), may hold values from 0.5 to 1.5
Outputs:
- residual_out: bfloat16 [2048, 4096], P('ctx', 'tp')
- mamba_out: bfloat16 [2048, 4096], P('ctx', 'tp')
The draws below stay inside these ranges and needn't reach their ends.
All inputs are finite; a program needn't handle non-finite values.
Results may differ from the reference program's by a relative error of at most 0.034.
Values may be sent and summed in bfloat16 or wider, within the bound.
A program may use at most 64 MiB of HBM per device.

```python
import math
import jax
import jax.numpy as jnp
from jax import lax

D = 4096
HQ = 16
KEY_VALUE_HEADS = 4
HEAD_SIZE = 128
MH = 64
P_SIZE = 64
N = 128
NG = 4
TOK_DEV = 256
TOKEN_COUNT = 2048
BLOCK = 128
GROUP = 4
HPG = 16
N_CTX = 8
N_TP = 4


def query_key_pair(key):
    base_key = jax.random.fold_in(key, 17)
    key_query, random_key_split = jax.random.split(base_key, 2)
    query_vals = jnp.clip(jax.random.normal(key_query, (TOKEN_COUNT, HQ * HEAD_SIZE), jnp.float32), -6.0, 6.0)
    random_key_values = jnp.clip(jax.random.normal(random_key_split, (TOKEN_COUNT, KEY_VALUE_HEADS, HEAD_SIZE), jnp.float32), -6.0, 6.0)
    return (query_vals, random_key_values)


def draw_queries(key, part):
    return query_key_pair(key)[0].astype(jnp.bfloat16)


def draw_key_heads(key, part):
    return query_key_pair(key)[1].astype(jnp.bfloat16)


def decay_pair(key):
    base_key = jax.random.fold_in(key, 29)
    key_kind, key_slow, key_fast, key_jitter = jax.random.split(base_key, 4)
    share = 5
    slow_heads = jax.random.randint(key_kind, (MH,), 0, 10) < share
    slow_rate = jax.random.uniform(key_slow, (MH,), jnp.float32, 0.2, 1.0) / TOKEN_COUNT
    fast_rate = jnp.exp(jax.random.uniform(key_fast, (MH,), jnp.float32, math.log(1.0 / 50.0), math.log(1.0 / 30.0)))
    rate = jnp.where(slow_heads, slow_rate, fast_rate)
    span = jnp.minimum(TOKEN_COUNT * 1.0, 1.0 / rate)
    step_size = jax.random.uniform(key_jitter, (MH,), jnp.float32, 0.7, 1.4) / (11.0 * jnp.sqrt(span))
    bias = jnp.log(jnp.expm1(step_size))
    log_rate = jnp.log(rate / step_size)
    return (bias, log_rate)


def draw_dt_bias(key, part):
    return decay_pair(key)[0]


def draw_decay_log(key, part):
    return decay_pair(key)[1]


def block_scale(stream_key, dims, shards, low, largest):
    def one(axis_at, parts):
        draws = jax.random.uniform(jax.random.fold_in(jax.random.fold_in(stream_key, 6), axis_at), (parts,), jnp.float32, low / len(shards), largest / len(shards))
        return jnp.repeat(jnp.exp(draws), dims[axis_at] // parts).reshape((-1,) + (1,) * (len(dims) - axis_at - 1))

    loudness = one(*shards[0])
    for cut in shards[1:]:
        loudness = loudness * one(*cut)
    return loudness


def bell_draw(stream_key, shape, spread, limit, cuts=(), kind=jnp.bfloat16):
    values = spread * jax.random.normal(stream_key, shape, jnp.float32)
    if cuts:
        values = values * block_scale(stream_key, shape, cuts, -0.22, 0.18)
    return jnp.clip(values, -limit, limit).astype(kind)


def setup_inputs(seed: int = 0) -> dict:
    seeds = jax.random.split(jax.random.key(seed), 13)
    return {
        "queries": draw_queries(jax.random.fold_in(seeds[12], 71), 0),
        "key_heads": draw_key_heads(jax.random.fold_in(seeds[12], 71), 0),
        "head_values": bell_draw(seeds[2], (TOKEN_COUNT, KEY_VALUE_HEADS, HEAD_SIZE), 1.0, 6.0, ((0, 8),)),
        "hidden": bell_draw(seeds[3], (TOKEN_COUNT, D), 0.1, 0.59765625, ((0, 8),)),
        "out_proj": bell_draw(seeds[4], (HQ * HEAD_SIZE, D), (HQ * HEAD_SIZE) ** -0.5, 0.125, ((0, 4),)),
        "norm_gain": jnp.clip(1.0 + 0.15 * jax.random.normal(seeds[5], (D,), jnp.float32), 0.25, 1.75),
        "x_proj": bell_draw(seeds[6], (D, MH * P_SIZE), (4 * D) ** -0.5, 0.046875, ((0, 8), (1, 4))),
        "bc_proj": bell_draw(seeds[7], (D, NG, 2 * N), D ** -0.5, 0.09375, ((0, 8),)),
        "dt_proj": bell_draw(seeds[8], (D, MH), D ** -0.5, 0.09375, ((0, 8), (1, 4))),
        "dt_bias": draw_dt_bias(jax.random.fold_in(seeds[12], 71), 0),
        "decay_log": draw_decay_log(jax.random.fold_in(seeds[12], 71), 0),
        "skip_gain": jnp.clip(0.5 + 1.0 * jax.random.uniform(seeds[11], (MH,), jnp.float32) ** block_scale(seeds[11], (MH,), ((0, 4),), -0.2, 0.2), 0.5, 1.5),
    }


def sequence_rows():
    position = jnp.arange(TOKEN_COUNT, dtype=jnp.int32)
    block = position // BLOCK
    offset = position % BLOCK
    device = jnp.where(block < N_CTX, block, 2 * N_CTX - 1 - block)
    within = jnp.where(block < N_CTX, offset, BLOCK + offset)
    return (device * TOK_DEV + within).astype(jnp.int32)

def row_positions():
    rows = jnp.arange(TOKEN_COUNT, dtype=jnp.int32)
    device = rows // TOK_DEV
    within = rows % TOK_DEV
    block = jnp.where(within < BLOCK, device, 2 * N_CTX - 1 - device)
    return (block * BLOCK + within % BLOCK).astype(jnp.int32)

def reference(queries, key_heads, head_values, hidden, out_proj, norm_gain, x_proj, bc_proj, dt_proj, dt_bias, decay_log, skip_gain):
    order = sequence_rows()
    back = row_positions()
    seq_q = queries[order].reshape(TOKEN_COUNT, HQ, HEAD_SIZE).astype(jnp.float32)
    seq_k = jnp.repeat(key_heads[order].astype(jnp.float32), GROUP, axis=1)
    seq_v = jnp.repeat(head_values[order].astype(jnp.float32), GROUP, axis=1)
    q_block = math.gcd(512, TOKEN_COUNT)
    key_pos = jnp.arange(TOKEN_COUNT, dtype=jnp.int32)

    def attend_block(index):
        start = index * q_block
        part_q = lax.dynamic_slice_in_dim(seq_q, start, q_block, 0)
        scores = jnp.einsum('qhd,khd->hqk', part_q, seq_k, precision=lax.Precision.HIGHEST) / math.sqrt(HEAD_SIZE)
        query_pos = start + jnp.arange(q_block, dtype=jnp.int32)
        allowed = (key_pos[None, :] <= query_pos[:, None])[None]
        top = lax.optimization_barrier(jnp.max(jnp.where(allowed, scores, -1e+30), axis=-1))
        weights = jnp.where(allowed, jnp.exp(scores - top[..., None]), 0.0)
        total = lax.optimization_barrier(jnp.sum(weights, axis=-1))
        rounded = lax.optimization_barrier(weights.astype(jnp.bfloat16)).astype(jnp.float32)
        mixed = jnp.einsum('hqk,khd->qhd', rounded, seq_v, precision=lax.Precision.HIGHEST)
        return (mixed / jnp.transpose(total)[:, :, None]).astype(jnp.bfloat16)
    attended = lax.map(attend_block, jnp.arange(TOKEN_COUNT // q_block, dtype=jnp.int32)).reshape(TOKEN_COUNT, HQ * HEAD_SIZE)
    head_cols = HQ * HEAD_SIZE // N_TP
    grouped_o = jnp.transpose(attended.reshape(TOKEN_COUNT, N_TP, head_cols), (1, 0, 2))
    grouped_w = out_proj.reshape(N_TP, head_cols, D)

    def add_group(running, pair):
        part = jnp.dot(pair[0], pair[1], preferred_element_type=jnp.float32)
        part = lax.optimization_barrier(part.astype(jnp.bfloat16)).astype(jnp.float32)
        return (running + part, None)
    attention_sum, _ = lax.scan(add_group, jnp.zeros((TOKEN_COUNT, D), jnp.float32), (grouped_o, grouped_w))
    residual = (hidden[order].astype(jnp.float32) + attention_sum).astype(jnp.bfloat16)
    as_float = residual.astype(jnp.float32)
    mean_square = lax.optimization_barrier(jnp.mean(as_float * as_float, axis=-1, keepdims=True))
    normed = (as_float * lax.rsqrt(mean_square + 1e-05) * norm_gain).astype(jnp.bfloat16)
    x_seq = lax.optimization_barrier(jnp.dot(normed, x_proj, preferred_element_type=jnp.float32).astype(jnp.bfloat16))
    bc_seq = lax.optimization_barrier(jnp.dot(normed, bc_proj.reshape(D, NG * 2 * N), preferred_element_type=jnp.float32).astype(jnp.bfloat16))
    bc_seq = bc_seq.astype(jnp.float32).reshape(TOKEN_COUNT, NG, 2 * N)
    step_sizes = jax.nn.softplus(jnp.dot(normed, dt_proj, preferred_element_type=jnp.float32) + dt_bias)
    rates = -jnp.exp(decay_log)
    inputs = x_seq.astype(jnp.float32).reshape(TOKEN_COUNT, MH, P_SIZE)

    def advance(state, items):
        x_now, b_now, c_now, step_now = items
        b_rows = jnp.repeat(b_now, HPG, axis=0)
        c_rows = jnp.repeat(c_now, HPG, axis=0)
        decay = jnp.exp(step_now * rates)
        state = decay[:, None, None] * state + (step_now[:, None] * x_now)[:, :, None] * b_rows[:, None, :]
        output = jnp.einsum('hpn,hn->hp', state, c_rows, precision=lax.Precision.HIGHEST) + skip_gain[:, None] * x_now
        return (state, output)
    _, outputs = lax.scan(advance, jnp.zeros((MH, P_SIZE, N), jnp.float32), (inputs, bc_seq[..., :N], bc_seq[..., N:], step_sizes))
    mamba = outputs.reshape(TOKEN_COUNT, MH * P_SIZE).astype(jnp.bfloat16)
    return (residual[back], mamba[back])
```

```python
import functools
import math

import jax
import jax.numpy as jnp
from jax import lax
from jax.experimental import pallas as pl
from jax.experimental.pallas import tpu as pltpu
from jax.sharding import PartitionSpec as P

MESH = pl.DeviceIdType.MESH
BF16 = jnp.bfloat16
F32 = jnp.float32
LANES = 128


class RingGather:
    def __init__(self, own, slot, n_ctx, halves, send, recv, local):
        self.slot, self.halves, self.own = slot, halves, own
        self.send, self.recv, self.local = send, recv, local
        me = lax.axis_index("ctx")
        self.me, self.core = me, me % 2
        chips = n_ctx // 2
        self.chips = chips
        self.steps = chips // 2
        self.width = math.isqrt(chips)
        chip = me // 2
        row = chip // self.width
        col = chip % self.width
        self.place = row * self.width + col + (row % 2) * (self.width - 1 - 2 * col)
        self.right = self.chip_at(1) * 2 + self.core
        self.left = self.chip_at(chips - 1) * 2 + self.core
        self.partner = (me // 2) * 2 + 1 - self.core
        self.sent = []

    def chip_at(self, ahead):
        place = (self.place + ahead) % self.chips
        row = place // self.width
        col = place % self.width
        return row * self.width + col + (row % 2) * (self.width - 1 - 2 * col)

    def neighbours(self):
        return [self.right, self.left, self.partner]

    def part(self, step, way):
        return None if step < self.steps else way

    def copy(self, src, dst, sem, to):
        return pltpu.make_async_remote_copy(
            src_ref=src,
            dst_ref=dst,
            send_sem=self.send.at[sem],
            recv_sem=self.recv.at[sem],
            device_id={"ctx": to},
            device_id_type=MESH,
        )

    def ring_sem(self, step, way):
        return 2 * (step - 1) + way

    def pair_sem(self, step, way):
        return 2 * self.steps + 1 + 2 * (step - 1) + way

    def start(self):
        self.keep = pltpu.make_async_copy(self.own, self.slot(self.me, None), self.local)
        self.keep.start()
        for way, to in ((0, self.right), (1, self.left)):
            part = self.part(1, way)
            src = self.own if part is None else self.halves(part)
            self.go(self.copy(src, self.slot(self.me, part), self.ring_sem(1, way), to))
        self.go(self.copy(self.own, self.slot(self.me, None), 2 * self.steps, self.partner))

    def go(self, copy):
        copy.start()
        self.sent.append(copy)

    def step(self, step):
        for way, to in ((0, self.right), (1, self.left)):
            ahead = self.chips - step if way == 0 else step
            shard = self.chip_at(ahead) * 2 + self.core
            place = self.slot(shard, self.part(step, way))
            self.copy(place, place, self.ring_sem(step, way), to).wait_recv()
            if step < self.steps:
                passed = self.slot(shard, self.part(step + 1, way))
                self.go(self.copy(passed, passed, self.ring_sem(step + 1, way), to))
            self.go(self.copy(place, place, self.pair_sem(step, way), self.partner))

    def finish(self):
        self.keep.wait()
        other = 1 - self.core
        place = self.slot(self.chip_at(0) * 2 + other, None)
        self.copy(place, place, 2 * self.steps, self.partner).wait_recv()
        for step in range(1, self.steps + 1):
            for way in (0, 1):
                ahead = self.chips - step if way == 0 else step
                shard = self.chip_at(ahead) * 2 + other
                place = self.slot(shard, self.part(step, way))
                self.copy(place, place, self.pair_sem(step, way), self.partner).wait_recv()

    def drain(self):
        for copy in self.sent:
            copy.wait_send()


class LineGather:
    def __init__(self, buffer, n_tp, send, recv):
        self.buffer, self.n_tp, self.send, self.recv = buffer, n_tp, send, recv
        self.me = lax.axis_index("tp")

    def copy(self, index, step, way, to):
        return pltpu.make_async_remote_copy(
            src_ref=self.buffer.at[index],
            dst_ref=self.buffer.at[index],
            send_sem=self.send.at[2 * (step - 1) + way],
            recv_sem=self.recv.at[2 * (step - 1) + way],
            device_id={"tp": to},
            device_id_type=MESH,
        )

    def launch(self, step):
        me = self.me

        @pl.when((me + 1 < self.n_tp) & (me - step + 1 >= 0))
        def _():
            self.copy(me - step + 1, step, 0, me + 1).start()

        @pl.when((me >= 1) & (me + step - 1 < self.n_tp))
        def _():
            self.copy(me + step - 1, step, 1, me - 1).start()

    def run(self, use):
        me = self.me
        for step in range(1, self.n_tp):

            @pl.when(me - step >= 0)
            def _():
                self.copy(me - step, step, 0, me).wait_recv()

            @pl.when(me + step < self.n_tp)
            def _():
                self.copy(me + step, step, 1, me).wait_recv()

            if step + 1 < self.n_tp:
                self.launch(step + 1)

            @pl.when(me - step >= 0)
            def _():
                use(me - step)

            @pl.when(me + step < self.n_tp)
            def _():
                use(me + step)

    def drain(self):
        me = self.me
        for step in range(1, self.n_tp):

            @pl.when((me + 1 < self.n_tp) & (me - step + 1 >= 0))
            def _():
                self.copy(me - step + 1, step, 0, me).wait_send()

            @pl.when((me >= 1) & (me + step - 1 < self.n_tp))
            def _():
                self.copy(me + step - 1, step, 1, me).wait_send()


def barrier_with(devices):
    barrier = pltpu.get_barrier_semaphore()
    for device in devices:
        pl.semaphore_signal(barrier, inc=1, device_id=device, device_id_type=MESH)
    pl.semaphore_wait(barrier, len(devices))


def front_kernel(
    n_ctx,
    n_tp,
    heads,
    widths,
    q_ref,
    kv_ref,
    hidden_ref,
    out_ref,
    gain_ref,
    w_ref,
    res_ref,
    x_ref,
    bc_ref,
    dt_ref,
    kv_all,
    w_all,
    o_all,
    o_full,
    att_all,
    res_all,
    hidden_mine,
    q_rows,
    scores,
    top,
    total,
    mixed,
    sums,
    proj,
    square,
    kv_send,
    kv_recv,
    o_send,
    o_recv,
    w_send,
    w_recv,
    t_send,
    t_recv,
    a_send,
    a_recv,
    r_send,
    r_recv,
    local,
):
    ctx = lax.axis_index("ctx")
    tp = lax.axis_index("tp")
    tok = q_ref.shape[0]
    half = tok // 2
    head_dim = kv_ref.shape[1] // 2
    cols = hidden_mine.shape[1]
    depth = w_ref.shape[0]
    slab = out_ref.shape[0]
    piece = o_all.shape[1] // n_ctx
    repeat = piece * n_ctx // slab

    def kv_slot(i, part):
        if part is None:
            return kv_all.at[pl.ds(pl.multiple_of(i * tok, tok), tok)]
        return kv_all.at[pl.ds(pl.multiple_of(i * tok + part * half, half), half)]

    def w_slot(i, part):
        if part is None:
            return w_all.at[pl.ds(pl.multiple_of(i * depth, depth), depth)]
        return w_all.at[pl.ds(pl.multiple_of(i * depth + part * (depth // 2), depth // 2), depth // 2)]

    def o_slot(i, part):
        rows = pl.ds(pl.multiple_of(i * piece, piece), piece)
        if part is None:
            return o_all.at[:, rows]
        return o_all.at[pl.ds(part * (n_tp // 2), n_tp // 2), rows]

    kv = RingGather(
        kv_ref, kv_slot, n_ctx, lambda part: kv_ref.at[pl.ds(part * half, half)],
        kv_send, kv_recv, local.at[0],
    )
    w = RingGather(
        w_ref, w_slot, n_ctx, lambda part: w_ref.at[pl.ds(part * (depth // 2), depth // 2)],
        w_send, w_recv, local.at[1],
    )
    o = RingGather(
        o_slot(ctx, None), o_slot, n_ctx, lambda part: o_slot(ctx, part),
        o_send, o_recv, local.at[2],
    )
    barrier_with(
        [{"ctx": to} for to in kv.neighbours()]
        + [{"tp": (tp + ahead) % n_tp} for ahead in range(1, n_tp)]
    )

    kv.start()
    my_rows = pl.ds(pl.multiple_of((ctx // repeat) * piece, piece), piece)
    my_place = pl.ds(pl.multiple_of(ctx * piece, piece), piece)

    def o_columns(t):
        return out_ref.at[my_rows, pl.ds(pl.multiple_of(t * cols, cols), cols)]

    swaps = []
    for ahead in range(1, n_tp):
        to = (tp + ahead) % n_tp
        swap = pltpu.make_async_remote_copy(
            src_ref=o_columns(to),
            dst_ref=o_all.at[tp, my_place],
            send_sem=t_send.at[ahead],
            recv_sem=t_recv.at[ahead],
            device_id={"tp": to},
            device_id_type=MESH,
        )
        swap.start()
        swaps.append(swap)
    keep_o = pltpu.make_async_copy(o_columns(tp), o_all.at[tp, my_place], local.at[3])
    keep_o.start()
    get_hidden = pltpu.make_async_copy(
        hidden_ref.at[:, pl.ds(pl.multiple_of(tp * cols, cols), cols)], hidden_mine, local.at[4]
    )
    get_hidden.start()

    for part in range(2):
        for head in range(heads):
            q_rows[part, head * half : (head + 1) * half, :] = q_ref[
                part * half : (part + 1) * half, head * head_dim : (head + 1) * head_dim
            ]
    top[...] = jnp.full_like(top, -1e30)
    total[...] = jnp.zeros_like(total)
    mixed[...] = jnp.zeros_like(mixed)

    for step in range(1, kv.steps + 1):
        kv.step(step)

    for ahead, swap in zip(range(1, n_tp), swaps):
        swap.wait_recv()
    keep_o.wait()
    for way, to in ((0, o.right), (1, o.left)):
        place = o_slot(ctx, o.part(1, way))
        o.go(o.copy(place, place, o.ring_sem(1, way), to))
    place = o_slot(ctx, None)
    o.go(o.copy(place, place, 2 * o.steps, o.partner))
    kv.finish()

    scale = 1.0 / math.sqrt(head_dim)
    rows = heads * half
    row_at = lax.broadcasted_iota(jnp.int32, (rows, half), 0) % half
    col_at = lax.broadcasted_iota(jnp.int32, (rows, half), 1)
    causal = col_at <= row_at

    def place_of(unit):
        late = (unit - ctx - 1 + n_ctx) // n_ctx
        shard = unit - late
        return late, shard, shard * tok + late * half

    def block_scores(part, start):
        keys = kv_all[pl.ds(pl.multiple_of(start, half), half), :head_dim]
        return lax.dot_general(
            q_rows[part], keys, (((1,), (1,)), ((), ())), preferred_element_type=F32
        ) * scale

    def early_scores(j, carry):
        found = block_scores(1, j * tok)
        scores[j] = found
        top[1] = jnp.maximum(top[1], found)
        return carry

    def mixed_scores(unit, carry):
        late, shard, start = place_of(unit)
        found = block_scores(late, start)
        found = jnp.where(causal | (shard != ctx), found, -1e30)
        scores[n_ctx + unit] = found
        top[late] = jnp.maximum(top[late], found)
        return carry

    lax.fori_loop(0, n_ctx, early_scores, 0)
    lax.fori_loop(0, n_ctx + 1, mixed_scores, 0)
    o.step(1)
    for part in range(2):
        top[part] = jnp.broadcast_to(jnp.max(top[part], axis=1, keepdims=True), (rows, half))

    def add_block(slot, part, start):
        weights = jnp.exp(scores[slot] - top[part])
        total[part] = total[part] + weights
        values = kv_all[pl.ds(pl.multiple_of(start, half), half), head_dim:]
        mixed[part] = mixed[part] + jnp.dot(weights.astype(BF16), values, preferred_element_type=F32)

    def early_values(j, carry):
        add_block(j, 1, j * tok)
        return carry

    def mixed_values(unit, carry):
        late, shard, start = place_of(unit)
        add_block(n_ctx + unit, late, start)
        return carry

    lax.fori_loop(0, n_ctx, early_values, 0)
    lax.fori_loop(0, n_ctx + 1, mixed_values, 0)
    for part in range(2):
        ended = (mixed[part] / jnp.sum(total[part], axis=1, keepdims=True)).astype(BF16)
        for head in range(heads):
            att_all[
                tp, part * half : (part + 1) * half, head * head_dim : (head + 1) * head_dim
            ] = ended[head * half : (head + 1) * half]

    attended = LineGather(att_all, n_tp, a_send, a_recv)
    attended.launch(1)
    for step in range(2, o.steps + 1):
        o.step(step)
    w.start()
    get_hidden.wait()
    other = 1 - o.core
    place = o_slot(o.chip_at(0) * 2 + other, None)
    o.copy(place, place, 2 * o.steps, o.partner).wait_recv()
    for step in range(1, o.steps + 1):
        for way in (0, 1):
            ahead = o.chips - step if way == 0 else step
            place = o_slot(o.chip_at(ahead) * 2 + other, o.part(step, way))
            o.copy(place, place, o.pair_sem(step, way), o.partner).wait_recv()
    if repeat > 1:
        for i in range(slab // piece):
            o_full[:, i * piece : (i + 1) * piece] = o_all[:, i * repeat * piece : (i * repeat + 1) * piece]
    weight = o_full if repeat > 1 else o_all

    sums[...] = jnp.zeros_like(sums)

    def add_heads(t):
        part = jnp.dot(att_all[t], weight[t], preferred_element_type=F32)
        sums[...] += part.astype(BF16).astype(F32)

    add_heads(tp)
    attended.run(add_heads)
    mine = (hidden_mine[...].astype(F32) + sums[...]).astype(BF16)
    res_ref[...] = mine
    res_all[tp] = mine
    residual = LineGather(res_all, n_tp, r_send, r_recv)
    residual.launch(1)

    for step in range(1, w.steps + 1):
        w.step(step)
    w.finish()
    proj[...] = jnp.zeros_like(proj)
    square[...] = jnp.zeros_like(square)

    def add_features(t):
        part = res_all[t].astype(F32)
        squares = part * part
        folded = squares[:, :LANES]
        for i in range(1, cols // LANES):
            folded = folded + squares[:, i * LANES : (i + 1) * LANES]
        square[...] += folded
        scaled = (part * gain_ref[t]).astype(BF16)
        proj[...] += jnp.dot(
            scaled,
            w_all[pl.ds(pl.multiple_of(t * cols, cols), cols), :],
            preferred_element_type=F32,
        )

    add_features(tp)
    residual.run(add_features)
    mean = jnp.sum(square[...], axis=1, keepdims=True) / (cols * n_tp)
    inverse = lax.rsqrt(mean + 1e-05)
    x_wide, bc_wide = widths
    x_ref[...] = (proj[:, :x_wide] * inverse).astype(BF16)
    bc_ref[...] = (proj[:, x_wide : x_wide + bc_wide] * inverse).astype(BF16)
    dt_ref[...] = proj[:, x_wide + bc_wide :] * inverse

    kv.drain()
    o.drain()
    w.drain()
    for swap in swaps:
        swap.wait_send()
    attended.drain()
    residual.drain()


def front(n_ctx, n_tp, queries, kv, hidden, out_proj, gain, weights, widths):
    tok, q_wide = queries.shape
    head_dim = kv.shape[1] // 2
    heads = q_wide // head_dim
    half = tok // 2
    cols = hidden.shape[1] // n_tp
    slab = out_proj.shape[0]
    piece = max(16, slab // n_ctx)
    repeat = piece * n_ctx // slab
    rows = heads * half
    ring = 4 * (n_ctx // 4) + 1
    line = 2 * (n_tp - 1)
    vmem = pl.BlockSpec(memory_space=pltpu.VMEM)
    hbm = pl.BlockSpec(memory_space=pl.ANY)
    wide = weights.shape[1]
    dma = pltpu.SemaphoreType.DMA
    return pl.pallas_call(
        functools.partial(front_kernel, n_ctx, n_tp, heads, widths),
        out_shape=(
            jax.ShapeDtypeStruct((tok, cols), BF16),
            jax.ShapeDtypeStruct((tok, widths[0]), BF16),
            jax.ShapeDtypeStruct((tok, widths[1]), BF16),
            jax.ShapeDtypeStruct((tok, wide - widths[0] - widths[1]), F32),
        ),
        in_specs=[vmem, vmem, hbm, hbm, vmem, hbm],
        out_specs=(vmem,) * 4,
        scratch_shapes=[
            pltpu.VMEM((n_ctx * tok, 2 * head_dim), BF16),
            pltpu.VMEM((n_ctx * weights.shape[0], wide), BF16),
            pltpu.VMEM((n_tp, n_ctx * piece, cols), BF16),
            pltpu.VMEM((n_tp, slab, cols) if repeat > 1 else (1, 16, LANES), BF16),
            pltpu.VMEM((n_tp, tok, q_wide), BF16),
            pltpu.VMEM((n_tp, tok, cols), BF16),
            pltpu.VMEM((tok, cols), BF16),
            pltpu.VMEM((2, rows, head_dim), BF16),
            pltpu.VMEM((2 * n_ctx + 1, rows, half), F32),
            pltpu.VMEM((2, rows, half), F32),
            pltpu.VMEM((2, rows, half), F32),
            pltpu.VMEM((2, rows, head_dim), F32),
            pltpu.VMEM((tok, cols), F32),
            pltpu.VMEM((tok, wide), F32),
            pltpu.VMEM((tok, LANES), F32),
            dma((ring,)),
            dma((ring,)),
            dma((ring,)),
            dma((ring,)),
            dma((ring,)),
            dma((ring,)),
            dma((n_tp,)),
            dma((n_tp,)),
            dma((line,)),
            dma((line,)),
            dma((line,)),
            dma((line,)),
            dma((5,)),
        ],
        compiler_params=pltpu.CompilerParams(
            collective_id=0, has_side_effects=True, vmem_limit_bytes=56 * 1024 * 1024
        ),
    )(queries, kv, hidden, out_proj, gain.reshape(n_tp, 1, cols), weights)


def exact_dot(a, b, dims):
    return lax.dot_general(
        a, b, (dims, ((), ())), precision=lax.Precision.HIGHEST, preferred_element_type=F32
    )


def mixer_kernel(
    n_ctx,
    m_local,
    x_ref,
    bc_ref,
    dt_ref,
    bias_ref,
    log_ref,
    skip_ref,
    y_ref,
    state_out,
    state_in,
    log_out,
    log_in,
    enter_out,
    enter_in,
    rows_in,
    grown,
    inner,
    s_send,
    s_recv,
    l_send,
    l_recv,
    e_send,
    e_recv,
):
    me = lax.axis_index("ctx")
    tok, wide = x_ref.shape
    half = tok // 2
    state = bc_ref.shape[1] // 2
    head_wide = wide // m_local
    share = wide // n_ctx
    barrier_with([{"ctx": (me + ahead) % n_ctx} for ahead in range(1, n_ctx)])

    spread = (
        lax.broadcasted_iota(jnp.int32, (LANES, wide), 1) // head_wide
        == lax.broadcasted_iota(jnp.int32, (LANES, wide), 0)
    ).astype(F32)
    across = lax.broadcasted_iota(jnp.int32, (half, half), 1)
    down = lax.broadcasted_iota(jnp.int32, (half, half), 0)
    causal = across <= down
    lower = causal.astype(F32)
    rates = -jnp.exp(log_ref[...])
    kept = []
    log_out[...] = jnp.zeros_like(log_out)
    for chunk in range(2):
        at = slice(chunk * half, (chunk + 1) * half)
        steps = jax.nn.softplus(dt_ref[at, :] + bias_ref[...])
        cumul = exact_dot(lower, steps * rates, ((1,), (0,)))
        last = cumul[half - 1 : half, :]
        log_out[chunk : chunk + 1, :] = last
        tail = exact_dot(jnp.exp(last - cumul) * steps, spread, ((1,), (0,)))
        weighted = (x_ref[at, :].astype(F32) * tail).astype(BF16)
        made = lax.dot_general(
            weighted, bc_ref[at, :state], (((0,), (0,)), ((), ())), preferred_element_type=F32
        ).astype(BF16)
        for i in range(n_ctx):
            state_out[i, chunk * share : (chunk + 1) * share, :] = made[i * share : (i + 1) * share]
        grown[at, :] = exact_dot(jnp.exp(cumul), spread, ((1,), (0,)))
        kept.append((cumul, steps))

    def transfer(src, dst, send, recv, ahead):
        return pltpu.make_async_remote_copy(
            src_ref=src,
            dst_ref=dst,
            send_sem=send.at[ahead],
            recv_sem=recv.at[ahead],
            device_id={"ctx": (me + ahead) % n_ctx},
            device_id_type=MESH,
        )

    copies = []
    for ahead in range(1, n_ctx):
        to = (me + ahead) % n_ctx
        for copy in (
            transfer(state_out.at[to], state_in.at[me], s_send, s_recv, ahead),
            transfer(log_out, log_in.at[me], l_send, l_recv, ahead),
        ):
            copy.start()
            copies.append(copy)
    state_in[me] = state_out[me]
    log_in[me] = log_out[...]

    for chunk in range(2):
        at = slice(chunk * half, (chunk + 1) * half)
        cumul, steps = kept[chunk]
        cumul_t, steps_t = cumul.T, steps.T
        gram = lax.dot_general(
            bc_ref[at, state:], bc_ref[at, :state], (((1,), (1,)), ((), ())),
            preferred_element_type=F32,
        )
        gram = jnp.where(causal, gram, 0.0)
        per = LANES // head_wide
        for pair in range(m_local // per):
            lanes = slice(pair * LANES, (pair + 1) * LANES)
            x_pair = x_ref[at, lanes]
            found = None
            for k in range(per):
                head = pair * per + k
                gap = jnp.where(causal, cumul[:, head : head + 1] - cumul_t[head : head + 1, :], 0.0)
                mixing = gram * jnp.exp(gap) * steps_t[head : head + 1, :]
                one = jnp.dot(mixing.astype(BF16), x_pair, preferred_element_type=F32)
                found = one if k == 0 else jnp.where(across // head_wide == k, one, found)
            inner[at, lanes] = found + skip_ref[:, lanes] * x_pair.astype(F32)

    for ahead in range(1, n_ctx):
        src = (me + n_ctx - ahead) % n_ctx
        transfer(state_out.at[src], state_in.at[src], s_send, s_recv, ahead).wait_recv()
        transfer(log_out, log_in.at[src], l_send, l_recv, ahead).wait_recv()

    chosen = (
        (me * share + lax.broadcasted_iota(jnp.int32, (share, LANES), 0)) // head_wide
        == lax.broadcasted_iota(jnp.int32, (share, LANES), 1)
    ).astype(F32)
    running = jnp.zeros((share, state), F32)
    for block in range(2 * n_ctx):
        chunk = block // n_ctx
        src = block if chunk == 0 else 2 * n_ctx - 1 - block
        rows = slice(chunk * share, (chunk + 1) * share)
        enter_out[src, rows, :] = running.astype(BF16)
        logs = jnp.sum(chosen * log_in[src, chunk : chunk + 1, :], axis=1, keepdims=True)
        running = jnp.exp(logs) * running + state_in[src, rows, :].astype(F32)

    for ahead in range(1, n_ctx):
        to = (me + ahead) % n_ctx
        copy = transfer(enter_out.at[to], enter_in.at[me], e_send, e_recv, ahead)
        copy.start()
        copies.append(copy)
    enter_in[me] = enter_out[me]
    for ahead in range(1, n_ctx):
        src = (me + n_ctx - ahead) % n_ctx
        transfer(enter_out.at[src], enter_in.at[src], e_send, e_recv, ahead).wait_recv()
    for chunk in range(2):
        at = slice(chunk * half, (chunk + 1) * half)
        for i in range(n_ctx):
            rows_in[i * share : (i + 1) * share, :] = enter_in[
                i, chunk * share : (chunk + 1) * share, :
            ].astype(F32)
        carried = lax.dot_general(
            bc_ref[at, state:], rows_in[...].astype(BF16), (((1,), (1,)), ((), ())),
            preferred_element_type=F32,
        )
        y_ref[at, :] = (inner[at, :] + grown[at, :] * carried).astype(BF16)
    for copy in copies:
        copy.wait_send()


def mixer(n_ctx, m_local, x, bc, dt, bias, logs, skip):
    tok, wide = x.shape
    state = bc.shape[1] // 2
    share = wide // n_ctx
    vmem = pl.BlockSpec(memory_space=pltpu.VMEM)
    dma = pltpu.SemaphoreType.DMA
    return pl.pallas_call(
        functools.partial(mixer_kernel, n_ctx, m_local),
        out_shape=jax.ShapeDtypeStruct((tok, wide), BF16),
        in_specs=[vmem] * 6,
        out_specs=vmem,
        scratch_shapes=[
            pltpu.VMEM((n_ctx, 2 * share, state), BF16),
            pltpu.VMEM((n_ctx, 2 * share, state), BF16),
            pltpu.VMEM((8, LANES), F32),
            pltpu.VMEM((n_ctx, 8, LANES), F32),
            pltpu.VMEM((n_ctx, 2 * share, state), BF16),
            pltpu.VMEM((n_ctx, 2 * share, state), BF16),
            pltpu.VMEM((wide, state), F32),
            pltpu.VMEM((tok, wide), F32),
            pltpu.VMEM((tok, wide), F32),
        ]
        + [dma((n_ctx,))] * 6,
        compiler_params=pltpu.CompilerParams(
            collective_id=1, has_side_effects=True, vmem_limit_bytes=32 * 1024 * 1024
        ),
    )(x, bc, dt, bias, logs, skip)


def body(
    queries,
    key_heads,
    head_values,
    hidden,
    out_proj,
    norm_gain,
    x_proj,
    bc_proj,
    dt_proj,
    dt_bias,
    decay_log,
    skip_gain,
):
    n_ctx = lax.axis_size("ctx")
    n_tp = lax.axis_size("tp")
    tp = lax.axis_index("tp")
    head_dim = key_heads.shape[2]
    q_local = queries.shape[1] // head_dim
    group = q_local * n_tp // key_heads.shape[1]
    m_local = skip_gain.shape[0]
    per_group = m_local * n_tp // bc_proj.shape[1]
    assert q_local <= group and m_local <= per_group
    kv_head = tp * q_local // group
    kv = jnp.concatenate(
        [
            lax.dynamic_index_in_dim(key_heads, kv_head, 1, False),
            lax.dynamic_index_in_dim(head_values, kv_head, 1, False),
        ],
        axis=1,
    )
    bc_mine = lax.dynamic_index_in_dim(bc_proj, tp * m_local // per_group, 1, False)
    pad = LANES - m_local
    weights = jnp.concatenate([x_proj, bc_mine, jnp.pad(dt_proj, ((0, 0), (0, pad)))], axis=1)
    widths = (x_proj.shape[1], bc_mine.shape[1])
    residual_out, x, bc, dt = front(
        n_ctx, n_tp, queries, kv, hidden, out_proj, norm_gain, weights, widths
    )
    bias = jnp.pad(dt_bias, (0, pad)).reshape(1, LANES)
    logs = jnp.pad(decay_log, (0, pad)).reshape(1, LANES)
    skip = jnp.repeat(skip_gain, x_proj.shape[1] // m_local).reshape(1, -1)
    mamba_out = mixer(n_ctx, m_local, x, bc, dt, bias, logs, skip)
    return (residual_out, mamba_out)


def solution(mesh):
    placed = (
        P("ctx", "tp"),
        P("ctx", None, None),
        P("ctx", None, None),
        P("ctx", None),
        P("tp", None),
        P(),
        P("ctx", "tp"),
        P("ctx", None, None),
        P("ctx", "tp"),
        P("tp"),
        P("tp"),
        P("tp"),
    )
    return jax.shard_map(
        body,
        mesh=mesh,
        in_specs=placed,
        out_specs=(P("ctx", "tp"), P("ctx", "tp")),
        check_vma=False,
    )
```

```python
import functools
import math

import jax
import jax.numpy as jnp
from jax import lax
from jax.experimental import pallas as pl
from jax.experimental.pallas import tpu as pltpu
from jax.sharding import PartitionSpec as P

MESH = pl.DeviceIdType.MESH
BF16 = jnp.bfloat16
F32 = jnp.float32
LANES = 128


class RingGather:
    def __init__(self, own, slot, n_ctx, halves, send, recv, local):
        self.slot, self.halves, self.own = slot, halves, own
        self.send, self.recv, self.local = send, recv, local
        me = lax.axis_index("ctx")
        self.me, self.core = me, me % 2
        chips = n_ctx // 2
        self.chips = chips
        self.steps = chips // 2
        self.width = math.isqrt(chips)
        chip = me // 2
        row = chip // self.width
        col = chip % self.width
        self.place = row * self.width + col + (row % 2) * (self.width - 1 - 2 * col)
        self.right = self.chip_at(1) * 2 + self.core
        self.left = self.chip_at(chips - 1) * 2 + self.core
        self.partner = (me // 2) * 2 + 1 - self.core
        self.sent = []

    def chip_at(self, ahead):
        place = (self.place + ahead) % self.chips
        row = place // self.width
        col = place % self.width
        return row * self.width + col + (row % 2) * (self.width - 1 - 2 * col)

    def neighbours(self):
        return [self.right, self.left, self.partner]

    def part(self, step, way):
        return None if step < self.steps else way

    def copy(self, src, dst, sem, to):
        return pltpu.make_async_remote_copy(
            src_ref=src,
            dst_ref=dst,
            send_sem=self.send.at[sem],
            recv_sem=self.recv.at[sem],
            device_id={"ctx": to},
            device_id_type=MESH,
        )

    def ring_sem(self, step, way):
        return 2 * (step - 1) + way

    def pair_sem(self, step, way):
        return 2 * self.steps + 1 + 2 * (step - 1) + way

    def start(self):
        if self.local is not None:
            self.keep = pltpu.make_async_copy(self.own, self.slot(self.me, None), self.local)
            self.keep.start()
        for way, to in ((0, self.right), (1, self.left)):
            part = self.part(1, way)
            src = self.own if part is None else self.halves(part)
            self.go(self.copy(src, self.slot(self.me, part), self.ring_sem(1, way), to))
        self.go(self.copy(self.own, self.slot(self.me, None), 2 * self.steps, self.partner))

    def go(self, copy):
        copy.start()
        self.sent.append(copy)

    def step(self, step):
        for way, to in ((0, self.right), (1, self.left)):
            ahead = self.chips - step if way == 0 else step
            shard = self.chip_at(ahead) * 2 + self.core
            place = self.slot(shard, self.part(step, way))
            self.copy(place, place, self.ring_sem(step, way), to).wait_recv()
            if step < self.steps:
                passed = self.slot(shard, self.part(step + 1, way))
                self.go(self.copy(passed, passed, self.ring_sem(step + 1, way), to))
            self.go(self.copy(place, place, self.pair_sem(step, way), self.partner))

    def finish(self):
        if self.local is not None:
            self.keep.wait()
        other = 1 - self.core
        place = self.slot(self.chip_at(0) * 2 + other, None)
        self.copy(place, place, 2 * self.steps, self.partner).wait_recv()
        for step in range(1, self.steps + 1):
            for way in (0, 1):
                ahead = self.chips - step if way == 0 else step
                shard = self.chip_at(ahead) * 2 + other
                place = self.slot(shard, self.part(step, way))
                self.copy(place, place, self.pair_sem(step, way), self.partner).wait_recv()

    def drain(self):
        for copy in self.sent:
            copy.wait_send()


class LineGather:
    def __init__(self, buffer, n_tp, send, recv):
        self.buffer, self.n_tp, self.send, self.recv = buffer, n_tp, send, recv
        self.me = lax.axis_index("tp")

    def copy(self, index, step, way, to):
        return pltpu.make_async_remote_copy(
            src_ref=self.buffer.at[index],
            dst_ref=self.buffer.at[index],
            send_sem=self.send.at[2 * (step - 1) + way],
            recv_sem=self.recv.at[2 * (step - 1) + way],
            device_id={"tp": to},
            device_id_type=MESH,
        )

    def launch(self, step):
        me = self.me

        @pl.when((me + 1 < self.n_tp) & (me - step + 1 >= 0))
        def _():
            self.copy(me - step + 1, step, 0, me + 1).start()

        @pl.when((me >= 1) & (me + step - 1 < self.n_tp))
        def _():
            self.copy(me + step - 1, step, 1, me - 1).start()

    def arrive(self, step):
        me = self.me

        @pl.when(me - step >= 0)
        def _():
            self.copy(me - step, step, 0, me).wait_recv()

        @pl.when(me + step < self.n_tp)
        def _():
            self.copy(me + step, step, 1, me).wait_recv()

        if step + 1 < self.n_tp:
            self.launch(step + 1)

    def use(self, step, take):
        me = self.me

        @pl.when(me - step >= 0)
        def _():
            take(me - step)

        @pl.when(me + step < self.n_tp)
        def _():
            take(me + step)

    def drain(self):
        me = self.me
        for step in range(1, self.n_tp):

            @pl.when((me + 1 < self.n_tp) & (me - step + 1 >= 0))
            def _():
                self.copy(me - step + 1, step, 0, me).wait_send()

            @pl.when((me >= 1) & (me + step - 1 < self.n_tp))
            def _():
                self.copy(me + step - 1, step, 1, me).wait_send()


def barrier_with(devices):
    barrier = pltpu.get_barrier_semaphore()
    for device in devices:
        pl.semaphore_signal(barrier, inc=1, device_id=device, device_id_type=MESH)
    pl.semaphore_wait(barrier, len(devices))


CHUNKS = 4


def whole_kernel(
    n_ctx,
    n_tp,
    heads,
    m_local,
    q_ref,
    kv_ref,
    hidden_ref,
    out_ref,
    gain_ref,
    x_proj_ref,
    bc_proj_ref,
    dt_proj_ref,
    bias_ref,
    log_ref,
    skip_ref,
    res_ref,
    y_ref,
    kv_all,
    x_all,
    bc_all,
    dt_all,
    o_all,
    o_full,
    att_all,
    res_all,
    hidden_mine,
    q_rows,
    scores,
    top,
    total,
    mixed,
    sums,
    x_sum,
    bc_sum,
    dt_sum,
    square,
    x_low,
    bc_low,
    mixer_scratch,
    ring_send,
    ring_recv,
    t_send,
    t_recv,
    d_send,
    d_recv,
    a_send,
    a_recv,
    r_send,
    r_recv,
    local,
):
    ctx = lax.axis_index("ctx")
    tp = lax.axis_index("tp")
    tok = q_ref.shape[0]
    half = tok // 2
    head_dim = kv_ref.shape[1] // 2
    cols = hidden_mine.shape[1]
    depth = x_proj_ref.shape[0]
    slab = out_ref.shape[0]
    piece = o_all.shape[1] // n_ctx
    repeat = piece * n_ctx // slab

    def row_gather(index, own, everyone, first, count):
        whole = own.shape[0]

        def slot(i, part):
            start, rows = (0, count) if part is None else (part * (count // 2), count // 2)
            return everyone.at[pl.ds(pl.multiple_of(i * whole + (first + start), rows), rows)]

        return RingGather(
            own.at[pl.ds(first, count)],
            slot,
            n_ctx,
            lambda part: own.at[pl.ds(first + part * (count // 2), count // 2)],
            ring_send.at[index],
            ring_recv.at[index],
            local.at[index],
        )

    kv = row_gather(0, kv_ref, kv_all, 0, tok)
    bc = row_gather(1, bc_proj_ref, bc_all, 0, depth)
    chunk = depth // CHUNKS
    xs = [row_gather(2 + i, x_proj_ref, x_all, i * chunk, chunk) for i in range(CHUNKS)]
    weights = xs + [bc]

    def o_slot(i, part):
        rows = pl.ds(pl.multiple_of(i * piece, piece), piece)
        if part is None:
            return o_all.at[pl.ds(1, n_tp - 1), rows]
        return o_all.at[pl.ds(1, n_tp - 1), rows, pl.ds(part * (cols // 2), cols // 2)]

    o = RingGather(
        o_slot(ctx, None), o_slot, n_ctx, lambda part: o_slot(ctx, part),
        ring_send.at[2 + CHUNKS], ring_recv.at[2 + CHUNKS], None,
    )
    barrier_with(
        [{"ctx": (ctx + ahead) % n_ctx} for ahead in range(1, n_ctx)]
        + [{"tp": (tp + ahead) % n_tp} for ahead in range(1, n_tp)]
    )

    kv.start()
    my_rows = pl.ds(pl.multiple_of((ctx // repeat) * piece, piece), piece)
    my_place = pl.ds(pl.multiple_of(ctx * piece, piece), piece)

    swaps = []
    for ahead in range(1, n_tp):
        to = (tp + ahead) % n_tp
        swap = pltpu.make_async_remote_copy(
            src_ref=out_ref.at[my_rows, pl.ds(pl.multiple_of(to * cols, cols), cols)],
            dst_ref=o_all.at[n_tp - ahead, my_place],
            send_sem=t_send.at[ahead],
            recv_sem=t_recv.at[ahead],
            device_id={"tp": to},
            device_id_type=MESH,
        )
        swap.start()
        swaps.append(swap)
    my_cols = pl.ds(pl.multiple_of(tp * cols, cols), cols)
    keep_o = pltpu.make_async_copy(
        out_ref.at[:, my_cols], o_all.at[0, pl.ds(0, slab)], local.at[2 + CHUNKS]
    )
    keep_o.start()
    get_hidden = pltpu.make_async_copy(
        hidden_ref.at[:, my_cols], hidden_mine, local.at[3 + CHUNKS]
    )
    get_hidden.start()

    for part in range(2):
        for head in range(heads):
            q_rows[part, head * half : (head + 1) * half, :] = q_ref[
                part * half : (part + 1) * half, head * head_dim : (head + 1) * head_dim
            ]
    top[...] = jnp.full_like(top, -1e30)
    total[...] = jnp.zeros_like(total)
    mixed[...] = jnp.zeros_like(mixed)

    for step in range(1, kv.steps + 1):
        kv.step(step)
    xs[0].start()
    dt_all[ctx] = dt_proj_ref[...]
    dts = []
    for ahead in range(1, n_ctx):
        copy = pltpu.make_async_remote_copy(
            src_ref=dt_proj_ref,
            dst_ref=dt_all.at[ctx],
            send_sem=d_send.at[ahead],
            recv_sem=d_recv.at[ahead],
            device_id={"ctx": (ctx + ahead) % n_ctx},
            device_id_type=MESH,
        )
        copy.start()
        dts.append(copy)
    kv.finish()

    scale = 1.0 / math.sqrt(head_dim)
    rows = heads * half
    row_at = lax.broadcasted_iota(jnp.int32, (rows, half), 0) % half
    col_at = lax.broadcasted_iota(jnp.int32, (rows, half), 1)
    causal = col_at <= row_at

    def place_of(unit):
        late = (unit - ctx - 1 + n_ctx) // n_ctx
        shard = unit - late
        return late, shard, shard * tok + late * half

    def block_scores(part, start):
        keys = kv_all[pl.ds(pl.multiple_of(start, half), half), :head_dim]
        return lax.dot_general(
            q_rows[part], keys, (((1,), (1,)), ((), ())), preferred_element_type=F32
        ) * scale

    def early_scores(j, carry):
        found = block_scores(1, j * tok)
        scores[j] = found
        top[1] = jnp.maximum(top[1], found)
        return carry

    def mixed_scores(unit, carry):
        late, shard, start = place_of(unit)
        found = block_scores(late, start)
        found = jnp.where(causal | (shard != ctx), found, -1e30)
        scores[n_ctx + unit] = found
        top[late] = jnp.maximum(top[late], found)
        return carry

    lax.fori_loop(0, n_ctx, early_scores, 0)
    lax.fori_loop(0, n_ctx + 1, mixed_scores, 0)

    for swap in swaps:
        swap.wait_recv()
    o.start()
    xs[1].start()
    for part in range(2):
        top[part] = jnp.broadcast_to(jnp.max(top[part], axis=1, keepdims=True), (rows, half))

    def add_block(slot, part, start):
        found = jnp.exp(scores[slot] - top[part])
        total[part] = total[part] + found
        values = kv_all[pl.ds(pl.multiple_of(start, half), half), head_dim:]
        mixed[part] = mixed[part] + jnp.dot(found.astype(BF16), values, preferred_element_type=F32)

    def early_values(j, carry):
        add_block(j, 1, j * tok)
        return carry

    def mixed_values(unit, carry):
        late, shard, start = place_of(unit)
        add_block(n_ctx + unit, late, start)
        return carry

    lax.fori_loop(0, n_ctx, early_values, 0)
    lax.fori_loop(0, n_ctx + 1, mixed_values, 0)
    for part in range(2):
        ended = (mixed[part] / jnp.sum(total[part], axis=1, keepdims=True)).astype(BF16)
        for head in range(heads):
            att_all[
                tp, part * half : (part + 1) * half, head * head_dim : (head + 1) * head_dim
            ] = ended[head * half : (head + 1) * half]

    attended = LineGather(att_all, n_tp, a_send, a_recv)
    attended.launch(1)
    errands = [
        lambda: o.step(1),
        lambda: (xs[0].step(1), xs[2].start()),
        lambda: (xs[1].step(1), xs[3].start()),
    ]
    errands += [functools.partial(o.step, step) for step in range(2, o.steps + 1)]
    for at, step in enumerate(range(1, n_tp - 1)):
        attended.arrive(step)
        if at < 2:
            errands.pop(0)()
    while errands:
        errands.pop(0)()
    bc.start()
    get_hidden.wait()
    keep_o.wait()
    sums[...] = jnp.zeros_like(sums)

    def add_heads(t):
        slot = (t - tp + n_tp) % n_tp
        weight = o_full[slot] if repeat > 1 else o_all[slot]
        part = jnp.dot(att_all[t], weight, preferred_element_type=F32)
        sums[...] += part.astype(BF16).astype(F32)

    o.finish()
    if repeat > 1:
        o_full[0] = o_all[0, :slab]
        for i in range(slab // piece):
            o_full[1:, i * piece : (i + 1) * piece] = o_all[
                1:, i * repeat * piece : (i * repeat + 1) * piece
            ]
    add_heads(tp)
    for step in range(1, n_tp - 1):
        attended.use(step, add_heads)
    attended.arrive(n_tp - 1)
    attended.use(n_tp - 1, add_heads)
    mine = (hidden_mine[...].astype(F32) + sums[...]).astype(BF16)
    res_ref[...] = mine
    res_all[tp] = mine
    residual = LineGather(res_all, n_tp, r_send, r_recv)
    residual.launch(1)

    errands = []
    for step in range(2, bc.steps + 1):
        errands.append(lambda step=step: (xs[0].step(step), xs[1].step(step)))
    errands.append(lambda: xs[2].step(1))
    errands.append(lambda: xs[3].step(1))
    for step in range(2, bc.steps + 1):
        errands.append(lambda step=step: xs[2].step(step))
    errands.append(lambda: bc.step(1))
    for step in range(2, bc.steps + 1):
        errands.append(lambda step=step: xs[3].step(step))
    for step in range(2, bc.steps + 1):
        errands.append(lambda step=step: bc.step(step))
    share_of = -(-len(errands) // max(1, n_tp - 1))
    x_sum[...] = jnp.zeros_like(x_sum)
    bc_sum[...] = jnp.zeros_like(bc_sum)
    dt_sum[...] = jnp.zeros_like(dt_sum)
    square[...] = jnp.zeros_like(square)
    for step in range(1, n_tp - 1):
        for errand in errands[:share_of]:
            errand()
        errands = errands[share_of:]
        residual.arrive(step)
    for errand in errands:
        errand()
    for ahead, copy in enumerate(dts, 1):
        copy.wait_recv()
    for weight in weights:
        weight.finish()

    def add_features(t):
        part = res_all[t].astype(F32)
        squares = part * part
        folded = squares[:, :LANES]
        for i in range(1, cols // LANES):
            folded = folded + squares[:, i * LANES : (i + 1) * LANES]
        square[...] += folded
        scaled = (part * gain_ref[t]).astype(BF16)
        at = pl.ds(pl.multiple_of(t * cols, cols), cols)
        x_sum[...] += jnp.dot(scaled, x_all[at, :], preferred_element_type=F32)
        bc_sum[...] += jnp.dot(scaled, bc_all[at, :], preferred_element_type=F32)
        shards = cols // depth
        for i in range(shards):
            dt_sum[...] += lax.dot_general(
                scaled[:, i * depth : (i + 1) * depth], dt_all[t * shards + i],
                (((1,), (1,)), ((), ())), preferred_element_type=F32,
            )

    add_features(tp)
    for step in range(1, n_tp - 1):
        residual.use(step, add_features)
    residual.arrive(n_tp - 1)
    residual.use(n_tp - 1, add_features)
    mean = jnp.sum(square[...], axis=1, keepdims=True) / (cols * n_tp)
    inverse = lax.rsqrt(mean + 1e-05)
    x_low[...] = (x_sum[...] * inverse).astype(BF16)
    bc_low[...] = (bc_sum[...] * inverse).astype(BF16)
    dt = dt_sum[...] * inverse
    dt = jnp.concatenate([dt, jnp.zeros((tok, LANES - dt.shape[1]), F32)], axis=1)
    mixer(n_ctx, m_local, x_low, bc_low, dt, bias_ref, log_ref, skip_ref, y_ref, *mixer_scratch)

    for gather in [kv, o] + weights:
        gather.drain()
    for copy in swaps + dts:
        copy.wait_send()
    attended.drain()
    residual.drain()


def run_kernel(
    n_ctx, n_tp, queries, kv, hidden, out_proj, gain, x_proj, bc_proj, dt_proj, bias, logs, skip,
    m_local,
):
    tok, q_wide = queries.shape
    head_dim = kv.shape[1] // 2
    heads = q_wide // head_dim
    half = tok // 2
    cols = hidden.shape[1] // n_tp
    slab = out_proj.shape[0]
    piece = max(16, slab // n_ctx)
    repeat = piece * n_ctx // slab
    rows = heads * half
    ring = 4 * (n_ctx // 4) + 1
    line = 2 * (n_tp - 1)
    vmem = pl.BlockSpec(memory_space=pltpu.VMEM)
    hbm = pl.BlockSpec(memory_space=pl.ANY)
    depth, wide = x_proj.shape
    bc_wide = bc_proj.shape[1]
    state = bc_wide // 2
    share = wide // n_ctx
    dma = pltpu.SemaphoreType.DMA
    return pl.pallas_call(
        functools.partial(whole_kernel, n_ctx, n_tp, heads, m_local),
        out_shape=(
            jax.ShapeDtypeStruct((tok, cols), BF16),
            jax.ShapeDtypeStruct((tok, wide), BF16),
        ),
        in_specs=[vmem, vmem, hbm, hbm, vmem, hbm, hbm, vmem, vmem, vmem, vmem],
        out_specs=(vmem,) * 2,
        scratch_shapes=[
            pltpu.VMEM((n_ctx * tok, 2 * head_dim), BF16),
            pltpu.VMEM((n_ctx * depth, wide), BF16),
            pltpu.VMEM((n_ctx * depth, bc_wide), BF16),
            pltpu.VMEM((n_ctx,) + dt_proj.shape, BF16),
            pltpu.VMEM((n_tp, n_ctx * piece, cols), BF16),
            pltpu.VMEM((n_tp, slab, cols) if repeat > 1 else (1, 16, LANES), BF16),
            pltpu.VMEM((n_tp, tok, q_wide), BF16),
            pltpu.VMEM((n_tp, tok, cols), BF16),
            pltpu.VMEM((tok, cols), BF16),
            pltpu.VMEM((2, rows, head_dim), BF16),
            pltpu.VMEM((2 * n_ctx + 1, rows, half), F32),
            pltpu.VMEM((2, rows, half), F32),
            pltpu.VMEM((2, rows, half), F32),
            pltpu.VMEM((2, rows, head_dim), F32),
            pltpu.VMEM((tok, cols), F32),
            pltpu.VMEM((tok, wide), F32),
            pltpu.VMEM((tok, bc_wide), F32),
            pltpu.VMEM((tok, dt_proj.shape[0]), F32),
            pltpu.VMEM((tok, LANES), F32),
            pltpu.VMEM((tok, wide), BF16),
            pltpu.VMEM((tok, bc_wide), BF16),
            [
                pltpu.VMEM((n_ctx, 2 * share, state), BF16),
                pltpu.VMEM((n_ctx, 2 * share, state), BF16),
                pltpu.VMEM((8, LANES), F32),
                pltpu.VMEM((n_ctx, 8, LANES), F32),
                pltpu.VMEM((n_ctx, 2 * share, state), BF16),
                pltpu.VMEM((n_ctx, 2 * share, state), BF16),
                pltpu.VMEM((wide, state), F32),
                pltpu.VMEM((tok, wide), F32),
                pltpu.VMEM((tok, wide), F32),
            ]
            + [dma((n_ctx,))] * 6,
            dma((3 + CHUNKS, ring)),
            dma((3 + CHUNKS, ring)),
            dma((n_tp,)),
            dma((n_tp,)),
            dma((n_ctx,)),
            dma((n_ctx,)),
            dma((line,)),
            dma((line,)),
            dma((line,)),
            dma((line,)),
            dma((4 + CHUNKS,)),
        ],
        compiler_params=pltpu.CompilerParams(
            collective_id=0, has_side_effects=True, vmem_limit_bytes=56 * 1024 * 1024
        ),
    )(
        queries, kv, hidden, out_proj, gain.reshape(n_tp, 1, cols), x_proj, bc_proj, dt_proj,
        bias, logs, skip,
    )


def exact_dot(a, b, dims):
    return lax.dot_general(
        a, b, (dims, ((), ())), precision=lax.Precision.HIGHEST, preferred_element_type=F32
    )


def mixer(
    n_ctx,
    m_local,
    x_ref,
    bc_ref,
    dt,
    bias_ref,
    log_ref,
    skip_ref,
    y_ref,
    state_out,
    state_in,
    log_out,
    log_in,
    enter_out,
    enter_in,
    rows_in,
    grown,
    inner,
    s_send,
    s_recv,
    l_send,
    l_recv,
    e_send,
    e_recv,
):
    me = lax.axis_index("ctx")
    tok, wide = x_ref.shape
    half = tok // 2
    state = bc_ref.shape[1] // 2
    head_wide = wide // m_local
    share = wide // n_ctx

    spread = (
        lax.broadcasted_iota(jnp.int32, (LANES, wide), 1) // head_wide
        == lax.broadcasted_iota(jnp.int32, (LANES, wide), 0)
    ).astype(F32)
    across = lax.broadcasted_iota(jnp.int32, (half, half), 1)
    down = lax.broadcasted_iota(jnp.int32, (half, half), 0)
    causal = across <= down
    lower = causal.astype(F32)
    rates = -jnp.exp(log_ref[...])
    kept = []
    log_out[...] = jnp.zeros_like(log_out)
    for chunk in range(2):
        at = slice(chunk * half, (chunk + 1) * half)
        steps = jax.nn.softplus(dt[at] + bias_ref[...])
        cumul = exact_dot(lower, steps * rates, ((1,), (0,)))
        last = cumul[half - 1 : half, :]
        log_out[chunk : chunk + 1, :] = last
        tail = exact_dot(jnp.exp(last - cumul) * steps, spread, ((1,), (0,)))
        weighted = (x_ref[at, :].astype(F32) * tail).astype(BF16)
        made = lax.dot_general(
            weighted, bc_ref[at, :state], (((0,), (0,)), ((), ())), preferred_element_type=F32
        ).astype(BF16)
        for i in range(n_ctx):
            state_out[i, chunk * share : (chunk + 1) * share, :] = made[i * share : (i + 1) * share]
        grown[at, :] = exact_dot(jnp.exp(cumul), spread, ((1,), (0,)))
        kept.append((cumul, steps))

    def transfer(src, dst, send, recv, ahead):
        return pltpu.make_async_remote_copy(
            src_ref=src,
            dst_ref=dst,
            send_sem=send.at[ahead],
            recv_sem=recv.at[ahead],
            device_id={"ctx": (me + ahead) % n_ctx},
            device_id_type=MESH,
        )

    copies = []
    for ahead in range(1, n_ctx):
        to = (me + ahead) % n_ctx
        for copy in (
            transfer(state_out.at[to], state_in.at[me], s_send, s_recv, ahead),
            transfer(log_out, log_in.at[me], l_send, l_recv, ahead),
        ):
            copy.start()
            copies.append(copy)
    state_in[me] = state_out[me]
    log_in[me] = log_out[...]

    for chunk in range(2):
        at = slice(chunk * half, (chunk + 1) * half)
        cumul, steps = kept[chunk]
        cumul_t, steps_t = cumul.T, steps.T
        gram = lax.dot_general(
            bc_ref[at, state:], bc_ref[at, :state], (((1,), (1,)), ((), ())),
            preferred_element_type=F32,
        )
        gram = jnp.where(causal, gram, 0.0)
        per = LANES // head_wide
        for pair in range(m_local // per):
            lanes = slice(pair * LANES, (pair + 1) * LANES)
            x_pair = x_ref[at, lanes]
            found = None
            for k in range(per):
                head = pair * per + k
                gap = jnp.where(causal, cumul[:, head : head + 1] - cumul_t[head : head + 1, :], 0.0)
                mixing = gram * jnp.exp(gap) * steps_t[head : head + 1, :]
                one = jnp.dot(mixing.astype(BF16), x_pair, preferred_element_type=F32)
                found = one if k == 0 else jnp.where(across // head_wide == k, one, found)
            inner[at, lanes] = found + skip_ref[:, lanes] * x_pair.astype(F32)

    for ahead in range(1, n_ctx):
        src = (me + n_ctx - ahead) % n_ctx
        transfer(state_out.at[src], state_in.at[src], s_send, s_recv, ahead).wait_recv()
        transfer(log_out, log_in.at[src], l_send, l_recv, ahead).wait_recv()

    chosen = (
        (me * share + lax.broadcasted_iota(jnp.int32, (share, LANES), 0)) // head_wide
        == lax.broadcasted_iota(jnp.int32, (share, LANES), 1)
    ).astype(F32)
    running = jnp.zeros((share, state), F32)
    for block in range(2 * n_ctx):
        chunk = block // n_ctx
        src = block if chunk == 0 else 2 * n_ctx - 1 - block
        rows = slice(chunk * share, (chunk + 1) * share)
        enter_out[src, rows, :] = running.astype(BF16)
        logs = jnp.sum(chosen * log_in[src, chunk : chunk + 1, :], axis=1, keepdims=True)
        running = jnp.exp(logs) * running + state_in[src, rows, :].astype(F32)

    for ahead in range(1, n_ctx):
        to = (me + ahead) % n_ctx
        copy = transfer(enter_out.at[to], enter_in.at[me], e_send, e_recv, ahead)
        copy.start()
        copies.append(copy)
    enter_in[me] = enter_out[me]
    for ahead in range(1, n_ctx):
        src = (me + n_ctx - ahead) % n_ctx
        transfer(enter_out.at[src], enter_in.at[src], e_send, e_recv, ahead).wait_recv()
    for chunk in range(2):
        at = slice(chunk * half, (chunk + 1) * half)
        for i in range(n_ctx):
            rows_in[i * share : (i + 1) * share, :] = enter_in[
                i, chunk * share : (chunk + 1) * share, :
            ].astype(F32)
        carried = lax.dot_general(
            bc_ref[at, state:], rows_in[...].astype(BF16), (((1,), (1,)), ((), ())),
            preferred_element_type=F32,
        )
        y_ref[at, :] = (inner[at, :] + grown[at, :] * carried).astype(BF16)
    for copy in copies:
        copy.wait_send()


def body(
    queries,
    key_heads,
    head_values,
    hidden,
    out_proj,
    norm_gain,
    x_proj,
    bc_proj,
    dt_proj,
    dt_bias,
    decay_log,
    skip_gain,
):
    n_ctx = lax.axis_size("ctx")
    n_tp = lax.axis_size("tp")
    tp = lax.axis_index("tp")
    head_dim = key_heads.shape[2]
    q_local = queries.shape[1] // head_dim
    group = q_local * n_tp // key_heads.shape[1]
    m_local = skip_gain.shape[0]
    per_group = m_local * n_tp // bc_proj.shape[1]
    assert q_local <= group and m_local <= per_group
    kv_head = tp * q_local // group
    kv = jnp.concatenate(
        [
            lax.dynamic_index_in_dim(key_heads, kv_head, 1, False),
            lax.dynamic_index_in_dim(head_values, kv_head, 1, False),
        ],
        axis=1,
    )
    bc_mine = lax.dynamic_index_in_dim(bc_proj, tp * m_local // per_group, 1, False)
    rows = -(-m_local // 16) * 16
    dt_mine = jnp.pad(dt_proj.T, ((0, rows - m_local), (0, 0)))
    pad = LANES - m_local
    bias = jnp.pad(dt_bias, (0, pad)).reshape(1, LANES)
    logs = jnp.pad(decay_log, (0, pad)).reshape(1, LANES)
    skip = jnp.repeat(skip_gain, x_proj.shape[1] // m_local).reshape(1, -1)
    return run_kernel(
        n_ctx, n_tp, queries, kv, hidden, out_proj, norm_gain, x_proj, bc_mine, dt_mine,
        bias, logs, skip, m_local,
    )


def solution(mesh):
    placed = (
        P("ctx", "tp"),
        P("ctx", None, None),
        P("ctx", None, None),
        P("ctx", None),
        P("tp", None),
        P(),
        P("ctx", "tp"),
        P("ctx", None, None),
        P("ctx", "tp"),
        P("tp"),
        P("tp"),
        P("tp"),
    )
    return jax.shard_map(
        body,
        mesh=mesh,
        in_specs=placed,
        out_specs=(P("ctx", "tp"), P("ctx", "tp")),
        check_vma=False,
    )
```

```python
import functools
import math

import jax
import jax.numpy as jnp
from jax import lax
from jax.experimental import pallas as pl
from jax.experimental.pallas import tpu as pltpu
from jax.sharding import PartitionSpec as P

MESH = pl.DeviceIdType.MESH
BF16 = jnp.bfloat16
F32 = jnp.float32
LANES = 128


class RingGather:
    def __init__(self, own, slot, n_ctx, halves, send, recv, local):
        self.slot, self.halves, self.own = slot, halves, own
        self.send, self.recv, self.local = send, recv, local
        me = lax.axis_index("ctx")
        self.me, self.core = me, me % 2
        chips = n_ctx // 2
        self.chips = chips
        self.steps = chips // 2
        self.width = math.isqrt(chips)
        chip = me // 2
        row = chip // self.width
        col = chip % self.width
        self.place = row * self.width + col + (row % 2) * (self.width - 1 - 2 * col)
        self.right = self.chip_at(1) * 2 + self.core
        self.left = self.chip_at(chips - 1) * 2 + self.core
        self.partner = (me // 2) * 2 + 1 - self.core
        self.sent = []

    def chip_at(self, ahead):
        place = (self.place + ahead) % self.chips
        row = place // self.width
        col = place % self.width
        return row * self.width + col + (row % 2) * (self.width - 1 - 2 * col)

    def neighbours(self):
        return [self.right, self.left, self.partner]

    def part(self, step, way):
        return None if step < self.steps else way

    def copy(self, src, dst, sem, to):
        return pltpu.make_async_remote_copy(
            src_ref=src,
            dst_ref=dst,
            send_sem=self.send.at[sem],
            recv_sem=self.recv.at[sem],
            device_id={"ctx": to},
            device_id_type=MESH,
        )

    def ring_sem(self, step, way):
        return 2 * (step - 1) + way

    def pair_sem(self, step, way):
        return 2 * self.steps + 1 + 2 * (step - 1) + way

    def start(self):
        if self.local is not None:
            self.keep = pltpu.make_async_copy(self.own, self.slot(self.me, None), self.local)
            self.keep.start()
        for way, to in ((0, self.right), (1, self.left)):
            part = self.part(1, way)
            src = self.own if part is None else self.halves(part)
            self.go(self.copy(src, self.slot(self.me, part), self.ring_sem(1, way), to))
        self.go(self.copy(self.own, self.slot(self.me, None), 2 * self.steps, self.partner))

    def go(self, copy):
        copy.start()
        self.sent.append(copy)

    def step(self, step):
        for way, to in ((0, self.right), (1, self.left)):
            ahead = self.chips - step if way == 0 else step
            shard = self.chip_at(ahead) * 2 + self.core
            place = self.slot(shard, self.part(step, way))
            self.copy(place, place, self.ring_sem(step, way), to).wait_recv()
            if step < self.steps:
                passed = self.slot(shard, self.part(step + 1, way))
                self.go(self.copy(passed, passed, self.ring_sem(step + 1, way), to))
            self.go(self.copy(place, place, self.pair_sem(step, way), self.partner))

    def other_own(self):
        shard = self.chip_at(0) * 2 + 1 - self.core
        place = self.slot(shard, None)
        self.copy(place, place, 2 * self.steps, self.partner).wait_recv()

    def other_step(self, step):
        for way in (0, 1):
            ahead = self.chips - step if way == 0 else step
            shard = self.chip_at(ahead) * 2 + 1 - self.core
            place = self.slot(shard, self.part(step, way))
            self.copy(place, place, self.pair_sem(step, way), self.partner).wait_recv()

    def shards(self, step, core):
        far = [self.chip_at(self.chips - step), self.chip_at(step)]
        return [chip * 2 + core for chip in (far if step < self.steps else far[:1])]

    def finish(self):
        if self.local is not None:
            self.keep.wait()
        self.other_own()
        for step in range(1, self.steps + 1):
            self.other_step(step)

    def drain(self):
        for copy in self.sent:
            copy.wait_send()


class LineGather:
    def __init__(self, buffer, part, n_tp, send, recv):
        self.buffer, self.part, self.n_tp, self.send, self.recv = buffer, part, n_tp, send, recv
        self.me = lax.axis_index("tp")

    def copy(self, index, step, way, to):
        return pltpu.make_async_remote_copy(
            src_ref=self.buffer.at[index, self.part],
            dst_ref=self.buffer.at[index, self.part],
            send_sem=self.send.at[2 * (step - 1) + way],
            recv_sem=self.recv.at[2 * (step - 1) + way],
            device_id={"tp": to},
            device_id_type=MESH,
        )

    def launch(self, step):
        me = self.me

        @pl.when((me + 1 < self.n_tp) & (me - step + 1 >= 0))
        def _():
            self.copy(me - step + 1, step, 0, me + 1).start()

        @pl.when((me >= 1) & (me + step - 1 < self.n_tp))
        def _():
            self.copy(me + step - 1, step, 1, me - 1).start()

    def arrive(self, step):
        me = self.me

        @pl.when(me - step >= 0)
        def _():
            self.copy(me - step, step, 0, me).wait_recv()

        @pl.when(me + step < self.n_tp)
        def _():
            self.copy(me + step, step, 1, me).wait_recv()

        if step + 1 < self.n_tp:
            self.launch(step + 1)

    def use(self, step, take):
        me = self.me

        @pl.when(me - step >= 0)
        def _():
            take(me - step)

        @pl.when(me + step < self.n_tp)
        def _():
            take(me + step)

    def drain(self):
        me = self.me
        for step in range(1, self.n_tp):

            @pl.when((me + 1 < self.n_tp) & (me - step + 1 >= 0))
            def _():
                self.copy(me - step + 1, step, 0, me).wait_send()

            @pl.when((me >= 1) & (me + step - 1 < self.n_tp))
            def _():
                self.copy(me + step - 1, step, 1, me).wait_send()


def barrier_with(devices):
    barrier = pltpu.get_barrier_semaphore()
    for device in devices:
        pl.semaphore_signal(barrier, inc=1, device_id=device, device_id_type=MESH)
    pl.semaphore_wait(barrier, len(devices))


CHUNKS = 4


def whole_kernel(
    n_ctx,
    n_tp,
    heads,
    m_local,
    q_ref,
    kv_ref,
    hidden_ref,
    out_ref,
    gain_ref,
    x_proj_ref,
    bc_proj_ref,
    dt_proj_ref,
    bias_ref,
    log_ref,
    skip_ref,
    res_ref,
    y_ref,
    kv_all,
    x_all,
    bc_all,
    dt_all,
    o_all,
    o_full,
    att_all,
    res_all,
    hidden_mine,
    q_rows,
    scores,
    top,
    total,
    mixed,
    sums,
    x_sum,
    bc_sum,
    dt_sum,
    square,
    x_low,
    bc_low,
    mixer_scratch,
    ring_send,
    ring_recv,
    t_send,
    t_recv,
    d_send,
    d_recv,
    a_send,
    a_recv,
    r_send,
    r_recv,
    local,
):
    ctx = lax.axis_index("ctx")
    tp = lax.axis_index("tp")
    tok = q_ref.shape[0]
    half = tok // 2
    head_dim = kv_ref.shape[1] // 2
    cols = hidden_mine.shape[1]
    depth = x_proj_ref.shape[0]
    slab = out_ref.shape[0]
    piece = o_all.shape[1] // n_ctx
    repeat = piece * n_ctx // slab

    def row_gather(index, own, everyone, first, count):
        whole = own.shape[0]

        def slot(i, part):
            start, rows = (0, count) if part is None else (part * (count // 2), count // 2)
            return everyone.at[pl.ds(pl.multiple_of(i * whole + (first + start), rows), rows)]

        return RingGather(
            own.at[pl.ds(first, count)],
            slot,
            n_ctx,
            lambda part: own.at[pl.ds(first + part * (count // 2), count // 2)],
            ring_send.at[index],
            ring_recv.at[index],
            local.at[index],
        )

    kv = row_gather(0, kv_ref, kv_all, 0, tok)
    bc = row_gather(1, bc_proj_ref, bc_all, 0, depth)
    chunk = depth // CHUNKS
    xs = [row_gather(2 + i, x_proj_ref, x_all, i * chunk, chunk) for i in range(CHUNKS)]
    weights = xs + [bc]

    def o_slot(i, part):
        rows = pl.ds(pl.multiple_of(i * piece, piece), piece)
        if part is None:
            return o_all.at[pl.ds(1, n_tp - 1), rows]
        return o_all.at[pl.ds(1, n_tp - 1), rows, pl.ds(part * (cols // 2), cols // 2)]

    o = RingGather(
        o_slot(ctx, None), o_slot, n_ctx, lambda part: o_slot(ctx, part),
        ring_send.at[2 + CHUNKS], ring_recv.at[2 + CHUNKS], None,
    )
    barrier_with(
        [{"ctx": (ctx + ahead) % n_ctx} for ahead in range(1, n_ctx)]
        + [{"tp": (tp + ahead) % n_tp} for ahead in range(1, n_tp)]
    )

    kv.start()
    my_rows = pl.ds(pl.multiple_of((ctx // repeat) * piece, piece), piece)
    my_place = pl.ds(pl.multiple_of(ctx * piece, piece), piece)

    swaps = []
    for ahead in range(1, n_tp):
        to = (tp + ahead) % n_tp
        swap = pltpu.make_async_remote_copy(
            src_ref=out_ref.at[my_rows, pl.ds(pl.multiple_of(to * cols, cols), cols)],
            dst_ref=o_all.at[n_tp - ahead, my_place],
            send_sem=t_send.at[ahead],
            recv_sem=t_recv.at[ahead],
            device_id={"tp": to},
            device_id_type=MESH,
        )
        swap.start()
        swaps.append(swap)
    my_cols = pl.ds(pl.multiple_of(tp * cols, cols), cols)
    keep_o = pltpu.make_async_copy(
        out_ref.at[:, my_cols], o_all.at[0, pl.ds(0, slab)], local.at[2 + CHUNKS]
    )
    keep_o.start()
    get_hidden = pltpu.make_async_copy(
        hidden_ref.at[:, my_cols], hidden_mine, local.at[3 + CHUNKS]
    )
    get_hidden.start()

    for part in range(2):
        for head in range(heads):
            q_rows[part, head * half : (head + 1) * half, :] = q_ref[
                part * half : (part + 1) * half, head * head_dim : (head + 1) * head_dim
            ]
    top[...] = jnp.full_like(top, -1e30)
    total[...] = jnp.zeros_like(total)
    mixed[...] = jnp.zeros_like(mixed)

    scale = 1.0 / math.sqrt(head_dim)
    rows = heads * half
    row_at = lax.broadcasted_iota(jnp.int32, (rows, half), 0) % half
    col_at = lax.broadcasted_iota(jnp.int32, (rows, half), 1)
    causal = col_at <= row_at

    def late_of(shard):
        return (shard - ctx - 1 + n_ctx) // n_ctx

    def block_scores(keys_of, slot, part, start, masked):
        keys = keys_of[pl.ds(pl.multiple_of(start, half), half), :head_dim]
        found = lax.dot_general(
            q_rows[part], keys, (((1,), (1,)), ((), ())), preferred_element_type=F32
        ) * scale
        if masked:
            found = jnp.where(causal, found, -1e30)
        scores[slot] = found
        top[part] = jnp.maximum(top[part], found)

    def shard_scores(shard):
        block_scores(kv_all, shard, 1, shard * tok, False)
        late = late_of(shard)
        block_scores(kv_all, n_ctx + shard, late, shard * tok + late * half, False)

    block_scores(kv_ref, ctx, 1, 0, False)
    block_scores(kv_ref, n_ctx + ctx, 0, 0, True)
    block_scores(kv_ref, 2 * n_ctx, 1, half, True)
    kv.step(1)
    kv.other_own()
    shard_scores(kv.partner)
    for shard in kv.shards(1, kv.core):
        shard_scores(shard)
    for step in range(2, kv.steps + 1):
        kv.step(step)
        if step == 2:
            xs[0].start()
        kv.other_step(step - 1)
        for shard in kv.shards(step - 1, 1 - kv.core) + kv.shards(step, kv.core):
            shard_scores(shard)
    dt_all[ctx] = dt_proj_ref[...]
    dts = []
    for ahead in range(1, n_ctx):
        copy = pltpu.make_async_remote_copy(
            src_ref=dt_proj_ref,
            dst_ref=dt_all.at[ctx],
            send_sem=d_send.at[ahead],
            recv_sem=d_recv.at[ahead],
            device_id={"ctx": (ctx + ahead) % n_ctx},
            device_id_type=MESH,
        )
        copy.start()
        dts.append(copy)
    kv.other_step(kv.steps)
    for shard in kv.shards(kv.steps, 1 - kv.core):
        shard_scores(shard)
    kv.keep.wait()

    for swap in swaps:
        swap.wait_recv()
    o.start()
    for part in range(2):
        top[part] = jnp.broadcast_to(jnp.max(top[part], axis=1, keepdims=True), (rows, half))

    def add_block(slot, part, start):
        found = jnp.exp(scores[slot] - top[part])
        total[part] = total[part] + found
        values = kv_all[pl.ds(pl.multiple_of(start, half), half), head_dim:]
        mixed[part] = mixed[part] + jnp.dot(found.astype(BF16), values, preferred_element_type=F32)

    def early_early(j, carry):
        add_block(n_ctx + j, 0, j * tok)
        return carry

    def late_early(j, carry):
        add_block(j, 1, j * tok)
        return carry

    def late_late(j, carry):
        add_block(n_ctx + j, 1, j * tok + half)
        return carry

    def attend(part):
        ended = (mixed[part] / jnp.sum(total[part], axis=1, keepdims=True)).astype(BF16)
        for head in range(heads):
            att_all[tp, part, :, head * head_dim : (head + 1) * head_dim] = ended[
                head * half : (head + 1) * half
            ]

    attended = [LineGather(att_all, i, n_tp, a_send.at[i], a_recv.at[i]) for i in range(2)]
    lax.fori_loop(0, ctx + 1, early_early, 0)
    attend(0)
    attended[0].launch(1)
    lax.fori_loop(0, n_ctx, late_early, 0)
    lax.fori_loop(ctx + 1, n_ctx, late_late, 0)
    add_block(2 * n_ctx, 1, ctx * tok + half)
    attend(1)
    attended[1].launch(1)
    xs[1].start()
    errands = [
        lambda: o.step(1),
        lambda: (xs[0].step(1), xs[2].start(), o.step(2)),
        lambda: (xs[1].step(1), xs[3].start()),
    ]
    errands += [functools.partial(o.step, step) for step in range(3, o.steps + 1)]
    for at, step in enumerate(range(1, n_tp - 1)):
        attended[0].arrive(step)
        attended[1].arrive(step)
        if at < 2:
            errands.pop(0)()
    while errands:
        errands.pop(0)()
    bc.start()
    get_hidden.wait()
    keep_o.wait()

    def add_heads(t, part):
        slot = (t - tp + n_tp) % n_tp
        weight = o_full[slot] if repeat > 1 else o_all[slot]
        found = jnp.dot(att_all[t, part], weight, preferred_element_type=F32)
        sums[part] += found.astype(BF16).astype(F32)

    o.finish()
    if repeat > 1:
        o_full[0] = o_all[0, :slab]
        for i in range(slab // piece):
            o_full[1:, i * piece : (i + 1) * piece] = o_all[
                1:, i * repeat * piece : (i * repeat + 1) * piece
            ]
    residual = [LineGather(res_all, i, n_tp, r_send.at[i], r_recv.at[i]) for i in range(2)]
    sums[...] = jnp.zeros_like(sums)
    for part in range(2):
        take = functools.partial(add_heads, part=part)
        take(tp)
        for step in range(1, n_tp - 1):
            attended[part].use(step, take)
        attended[part].arrive(n_tp - 1)
        attended[part].use(n_tp - 1, take)
        at = slice(part * half, (part + 1) * half)
        mine = (hidden_mine[at, :].astype(F32) + sums[part]).astype(BF16)
        res_all[tp, part] = mine
        residual[part].launch(1)
        res_ref[at, :] = mine

    errands = []
    for step in range(2, bc.steps + 1):
        errands.append(lambda step=step: (xs[0].step(step), xs[1].step(step)))
    errands.append(lambda: xs[2].step(1))
    errands.append(lambda: xs[3].step(1))
    for step in range(2, bc.steps + 1):
        errands.append(lambda step=step: xs[2].step(step))
    errands.append(lambda: bc.step(1))
    for step in range(2, bc.steps + 1):
        errands.append(lambda step=step: xs[3].step(step))
    for step in range(2, bc.steps + 1):
        errands.append(lambda step=step: bc.step(step))
    share_of = -(-len(errands) // max(1, n_tp - 1))
    x_sum[...] = jnp.zeros_like(x_sum)
    bc_sum[...] = jnp.zeros_like(bc_sum)
    dt_sum[...] = jnp.zeros_like(dt_sum)
    square[...] = jnp.zeros_like(square)
    for step in range(1, n_tp - 1):
        for errand in errands[:share_of]:
            errand()
        errands = errands[share_of:]
        residual[0].arrive(step)
        residual[1].arrive(step)
    for errand in errands:
        errand()
    for ahead, copy in enumerate(dts, 1):
        copy.wait_recv()
    for weight in weights:
        weight.finish()

    def add_features(t):
        part = res_all[t].reshape(tok, cols).astype(F32)
        squares = part * part
        folded = squares[:, :LANES]
        for i in range(1, cols // LANES):
            folded = folded + squares[:, i * LANES : (i + 1) * LANES]
        square[...] += folded
        scaled = (part * gain_ref[t]).astype(BF16)
        at = pl.ds(pl.multiple_of(t * cols, cols), cols)
        x_sum[...] += jnp.dot(scaled, x_all[at, :], preferred_element_type=F32)
        bc_sum[...] += jnp.dot(scaled, bc_all[at, :], preferred_element_type=F32)
        shards = cols // depth
        for i in range(shards):
            dt_sum[...] += lax.dot_general(
                scaled[:, i * depth : (i + 1) * depth], dt_all[t * shards + i],
                (((1,), (1,)), ((), ())), preferred_element_type=F32,
            )

    add_features(tp)
    for step in range(1, n_tp - 1):
        residual[0].use(step, add_features)
    residual[0].arrive(n_tp - 1)
    residual[1].arrive(n_tp - 1)
    residual[0].use(n_tp - 1, add_features)
    mean = jnp.sum(square[...], axis=1, keepdims=True) / (cols * n_tp)
    inverse = lax.rsqrt(mean + 1e-05)
    x_low[...] = (x_sum[...] * inverse).astype(BF16)
    bc_low[...] = (bc_sum[...] * inverse).astype(BF16)
    dt = dt_sum[...] * inverse
    dt = jnp.concatenate([dt, jnp.zeros((tok, LANES - dt.shape[1]), F32)], axis=1)
    mixer(n_ctx, m_local, x_low, bc_low, dt, bias_ref, log_ref, skip_ref, y_ref, *mixer_scratch)

    for gather in [kv, o] + weights:
        gather.drain()
    for copy in swaps + dts:
        copy.wait_send()
    for line in attended + residual:
        line.drain()


def run_kernel(
    n_ctx, n_tp, queries, kv, hidden, out_proj, gain, x_proj, bc_proj, dt_proj, bias, logs, skip,
    m_local,
):
    tok, q_wide = queries.shape
    head_dim = kv.shape[1] // 2
    heads = q_wide // head_dim
    half = tok // 2
    cols = hidden.shape[1] // n_tp
    slab = out_proj.shape[0]
    piece = max(16, slab // n_ctx)
    repeat = piece * n_ctx // slab
    rows = heads * half
    ring = 4 * (n_ctx // 4) + 1
    line = 2 * (n_tp - 1)
    vmem = pl.BlockSpec(memory_space=pltpu.VMEM)
    hbm = pl.BlockSpec(memory_space=pl.ANY)
    depth, wide = x_proj.shape
    bc_wide = bc_proj.shape[1]
    state = bc_wide // 2
    share = wide // n_ctx
    dma = pltpu.SemaphoreType.DMA
    return pl.pallas_call(
        functools.partial(whole_kernel, n_ctx, n_tp, heads, m_local),
        out_shape=(
            jax.ShapeDtypeStruct((tok, cols), BF16),
            jax.ShapeDtypeStruct((tok, wide), BF16),
        ),
        in_specs=[vmem, vmem, hbm, hbm, vmem, hbm, hbm, vmem, vmem, vmem, vmem],
        out_specs=(vmem,) * 2,
        scratch_shapes=[
            pltpu.VMEM((n_ctx * tok, 2 * head_dim), BF16),
            pltpu.VMEM((n_ctx * depth, wide), BF16),
            pltpu.VMEM((n_ctx * depth, bc_wide), BF16),
            pltpu.VMEM((n_ctx,) + dt_proj.shape, BF16),
            pltpu.VMEM((n_tp, n_ctx * piece, cols), BF16),
            pltpu.VMEM((n_tp, slab, cols) if repeat > 1 else (1, 16, LANES), BF16),
            pltpu.VMEM((n_tp, 2, half, q_wide), BF16),
            pltpu.VMEM((n_tp, 2, half, cols), BF16),
            pltpu.VMEM((tok, cols), BF16),
            pltpu.VMEM((2, rows, head_dim), BF16),
            pltpu.VMEM((2 * n_ctx + 1, rows, half), F32),
            pltpu.VMEM((2, rows, half), F32),
            pltpu.VMEM((2, rows, half), F32),
            pltpu.VMEM((2, rows, head_dim), F32),
            pltpu.VMEM((2, half, cols), F32),
            pltpu.VMEM((tok, wide), F32),
            pltpu.VMEM((tok, bc_wide), F32),
            pltpu.VMEM((tok, dt_proj.shape[0]), F32),
            pltpu.VMEM((tok, LANES), F32),
            pltpu.VMEM((tok, wide), BF16),
            pltpu.VMEM((tok, bc_wide), BF16),
            [
                pltpu.VMEM((n_ctx, 2 * share, state), BF16),
                pltpu.VMEM((n_ctx, 2 * share, state), BF16),
                pltpu.VMEM((8, LANES), F32),
                pltpu.VMEM((n_ctx, 8, LANES), F32),
                pltpu.VMEM((n_ctx, 2 * share, state), BF16),
                pltpu.VMEM((n_ctx, 2 * share, state), BF16),
                pltpu.VMEM((wide, state), F32),
                pltpu.VMEM((tok, wide), F32),
                pltpu.VMEM((tok, wide), F32),
            ]
            + [dma((n_ctx,))] * 6,
            dma((3 + CHUNKS, ring)),
            dma((3 + CHUNKS, ring)),
            dma((n_tp,)),
            dma((n_tp,)),
            dma((n_ctx,)),
            dma((n_ctx,)),
            dma((2, line)),
            dma((2, line)),
            dma((2, line)),
            dma((2, line)),
            dma((4 + CHUNKS,)),
        ],
        compiler_params=pltpu.CompilerParams(
            collective_id=0, has_side_effects=True, vmem_limit_bytes=56 * 1024 * 1024
        ),
    )(
        queries, kv, hidden, out_proj, gain.reshape(n_tp, 1, cols), x_proj, bc_proj, dt_proj,
        bias, logs, skip,
    )


def exact_dot(a, b, dims):
    return lax.dot_general(
        a, b, (dims, ((), ())), precision=lax.Precision.HIGHEST, preferred_element_type=F32
    )


def mixer(
    n_ctx,
    m_local,
    x_ref,
    bc_ref,
    dt,
    bias_ref,
    log_ref,
    skip_ref,
    y_ref,
    state_out,
    state_in,
    log_out,
    log_in,
    enter_out,
    enter_in,
    rows_in,
    grown,
    inner,
    s_send,
    s_recv,
    l_send,
    l_recv,
    e_send,
    e_recv,
):
    me = lax.axis_index("ctx")
    tok, wide = x_ref.shape
    half = tok // 2
    state = bc_ref.shape[1] // 2
    head_wide = wide // m_local
    share = wide // n_ctx

    spread = (
        lax.broadcasted_iota(jnp.int32, (LANES, wide), 1) // head_wide
        == lax.broadcasted_iota(jnp.int32, (LANES, wide), 0)
    ).astype(F32).astype(BF16)
    spread = jnp.concatenate([spread, spread], axis=0)

    def widen(values):
        upper = values.astype(BF16)
        lower = (values - upper.astype(F32)).astype(BF16)
        return jnp.dot(
            jnp.concatenate([upper, lower], axis=1), spread, preferred_element_type=F32
        )

    across = lax.broadcasted_iota(jnp.int32, (half, half), 1)
    down = lax.broadcasted_iota(jnp.int32, (half, half), 0)
    causal = across <= down
    lower = causal.astype(F32)
    rates = -jnp.exp(log_ref[...])
    kept = []
    log_out[...] = jnp.zeros_like(log_out)
    for chunk in range(2):
        at = slice(chunk * half, (chunk + 1) * half)
        steps = jax.nn.softplus(dt[at] + bias_ref[...])
        cumul = exact_dot(lower, steps * rates, ((1,), (0,)))
        last = cumul[half - 1 : half, :]
        log_out[chunk : chunk + 1, :] = last
        tail = widen(jnp.exp(last - cumul) * steps)
        weighted = (x_ref[at, :].astype(F32) * tail).astype(BF16)
        made = lax.dot_general(
            weighted, bc_ref[at, :state], (((0,), (0,)), ((), ())), preferred_element_type=F32
        ).astype(BF16)
        for i in range(n_ctx):
            state_out[i, chunk * share : (chunk + 1) * share, :] = made[i * share : (i + 1) * share]
        kept.append((cumul, steps))

    def transfer(src, dst, send, recv, ahead):
        return pltpu.make_async_remote_copy(
            src_ref=src,
            dst_ref=dst,
            send_sem=send.at[ahead],
            recv_sem=recv.at[ahead],
            device_id={"ctx": (me + ahead) % n_ctx},
            device_id_type=MESH,
        )

    copies = []
    for ahead in range(1, n_ctx):
        to = (me + ahead) % n_ctx
        for copy in (
            transfer(state_out.at[to], state_in.at[me], s_send, s_recv, ahead),
            transfer(log_out, log_in.at[me], l_send, l_recv, ahead),
        ):
            copy.start()
            copies.append(copy)
    state_in[me] = state_out[me]
    log_in[me] = log_out[...]

    skip = widen(jnp.broadcast_to(skip_ref[...], (16, LANES)))[:1]
    for chunk in range(2):
        at = slice(chunk * half, (chunk + 1) * half)
        cumul, steps = kept[chunk]
        grown[at, :] = widen(jnp.exp(cumul))
        cumul_t, steps_t = cumul.T, steps.T
        gram = lax.dot_general(
            bc_ref[at, state:], bc_ref[at, :state], (((1,), (1,)), ((), ())),
            preferred_element_type=F32,
        )
        gram = jnp.where(causal, gram, 0.0)
        per = LANES // head_wide
        for pair in range(m_local // per):
            lanes = slice(pair * LANES, (pair + 1) * LANES)
            x_pair = x_ref[at, lanes]
            found = None
            for k in range(per):
                head = pair * per + k
                gap = jnp.where(causal, cumul[:, head : head + 1] - cumul_t[head : head + 1, :], 0.0)
                mixing = gram * jnp.exp(gap) * steps_t[head : head + 1, :]
                one = jnp.dot(mixing.astype(BF16), x_pair, preferred_element_type=F32)
                found = one if k == 0 else jnp.where(across // head_wide == k, one, found)
            inner[at, lanes] = found + skip[:, lanes] * x_pair.astype(F32)

    for ahead in range(1, n_ctx):
        src = (me + n_ctx - ahead) % n_ctx
        transfer(state_out.at[src], state_in.at[src], s_send, s_recv, ahead).wait_recv()
        transfer(log_out, log_in.at[src], l_send, l_recv, ahead).wait_recv()

    chosen = (
        (me * share + lax.broadcasted_iota(jnp.int32, (share, LANES), 0)) // head_wide
        == lax.broadcasted_iota(jnp.int32, (share, LANES), 1)
    ).astype(F32)
    running = jnp.zeros((share, state), F32)
    for block in range(2 * n_ctx):
        chunk = block // n_ctx
        src = block if chunk == 0 else 2 * n_ctx - 1 - block
        rows = slice(chunk * share, (chunk + 1) * share)
        enter_out[src, rows, :] = running.astype(BF16)
        logs = jnp.sum(chosen * log_in[src, chunk : chunk + 1, :], axis=1, keepdims=True)
        running = jnp.exp(logs) * running + state_in[src, rows, :].astype(F32)

    for ahead in range(1, n_ctx):
        to = (me + ahead) % n_ctx
        copy = transfer(enter_out.at[to], enter_in.at[me], e_send, e_recv, ahead)
        copy.start()
        copies.append(copy)
    enter_in[me] = enter_out[me]
    for ahead in range(1, n_ctx):
        src = (me + n_ctx - ahead) % n_ctx
        transfer(enter_out.at[src], enter_in.at[src], e_send, e_recv, ahead).wait_recv()
    for chunk in range(2):
        at = slice(chunk * half, (chunk + 1) * half)
        for i in range(n_ctx):
            rows_in[i * share : (i + 1) * share, :] = enter_in[
                i, chunk * share : (chunk + 1) * share, :
            ].astype(F32)
        carried = lax.dot_general(
            bc_ref[at, state:], rows_in[...].astype(BF16), (((1,), (1,)), ((), ())),
            preferred_element_type=F32,
        )
        y_ref[at, :] = (inner[at, :] + grown[at, :] * carried).astype(BF16)
    for copy in copies:
        copy.wait_send()


def body(
    queries,
    key_heads,
    head_values,
    hidden,
    out_proj,
    norm_gain,
    x_proj,
    bc_proj,
    dt_proj,
    dt_bias,
    decay_log,
    skip_gain,
):
    n_ctx = lax.axis_size("ctx")
    n_tp = lax.axis_size("tp")
    tp = lax.axis_index("tp")
    head_dim = key_heads.shape[2]
    q_local = queries.shape[1] // head_dim
    group = q_local * n_tp // key_heads.shape[1]
    m_local = skip_gain.shape[0]
    per_group = m_local * n_tp // bc_proj.shape[1]
    assert q_local <= group and m_local <= per_group
    kv_head = tp * q_local // group
    kv = jnp.concatenate(
        [
            lax.dynamic_index_in_dim(key_heads, kv_head, 1, False),
            lax.dynamic_index_in_dim(head_values, kv_head, 1, False),
        ],
        axis=1,
    )
    bc_mine = lax.dynamic_index_in_dim(bc_proj, tp * m_local // per_group, 1, False)
    rows = -(-m_local // 16) * 16
    dt_mine = jnp.pad(dt_proj.T, ((0, rows - m_local), (0, 0)))
    pad = LANES - m_local
    bias = jnp.pad(dt_bias, (0, pad)).reshape(1, LANES)
    logs = jnp.pad(decay_log, (0, pad)).reshape(1, LANES)
    skip = jnp.pad(skip_gain, (0, pad)).reshape(1, LANES)
    return run_kernel(
        n_ctx, n_tp, queries, kv, hidden, out_proj, norm_gain, x_proj, bc_mine, dt_mine,
        bias, logs, skip, m_local,
    )


def solution(mesh):
    placed = (
        P("ctx", "tp"),
        P("ctx", None, None),
        P("ctx", None, None),
        P("ctx", None),
        P("tp", None),
        P(),
        P("ctx", "tp"),
        P("ctx", None, None),
        P("ctx", "tp"),
        P("tp"),
        P("tp"),
        P("tp"),
    )
    return jax.shard_map(
        body,
        mesh=mesh,
        in_specs=placed,
        out_specs=(P("ctx", "tp"), P("ctx", "tp")),
        check_vma=False,
    )
```

```python
import functools
import math

import jax
import jax.numpy as jnp
from jax import lax
from jax.experimental import pallas as pl
from jax.experimental.pallas import tpu as pltpu
from jax.sharding import PartitionSpec as P

MESH = pl.DeviceIdType.MESH
BF16 = jnp.bfloat16
F32 = jnp.float32
LANES = 128


class RingGather:
    def __init__(self, own, slot, n_ctx, halves, send, recv, local):
        self.slot, self.halves, self.own = slot, halves, own
        self.send, self.recv, self.local = send, recv, local
        me = lax.axis_index("ctx")
        self.me, self.core = me, me % 2
        chips = n_ctx // 2
        self.chips = chips
        self.steps = chips // 2
        self.width = math.isqrt(chips)
        chip = me // 2
        row = chip // self.width
        col = chip % self.width
        self.place = row * self.width + col + (row % 2) * (self.width - 1 - 2 * col)
        self.right = self.chip_at(1) * 2 + self.core
        self.left = self.chip_at(chips - 1) * 2 + self.core
        self.partner = (me // 2) * 2 + 1 - self.core
        self.sent = []

    def chip_at(self, ahead):
        place = (self.place + ahead) % self.chips
        row = place // self.width
        col = place % self.width
        return row * self.width + col + (row % 2) * (self.width - 1 - 2 * col)

    def neighbours(self):
        return [self.right, self.left, self.partner]

    def part(self, step, way):
        return None if step < self.steps else way

    def copy(self, src, dst, sem, to):
        return pltpu.make_async_remote_copy(
            src_ref=src,
            dst_ref=dst,
            send_sem=self.send.at[sem],
            recv_sem=self.recv.at[sem],
            device_id={"ctx": to},
            device_id_type=MESH,
        )

    def ring_sem(self, step, way):
        return 2 * (step - 1) + way

    def pair_sem(self, step, way):
        return 2 * self.steps + 1 + 2 * (step - 1) + way

    def start(self):
        if self.local is not None:
            self.keep = pltpu.make_async_copy(self.own, self.slot(self.me, None), self.local)
            self.keep.start()
        for way, to in ((0, self.right), (1, self.left)):
            part = self.part(1, way)
            src = self.own if part is None else self.halves(part)
            self.go(self.copy(src, self.slot(self.me, part), self.ring_sem(1, way), to))
        self.go(self.copy(self.own, self.slot(self.me, None), 2 * self.steps, self.partner))

    def go(self, copy):
        copy.start()
        self.sent.append(copy)

    def step(self, step):
        for way, to in ((0, self.right), (1, self.left)):
            ahead = self.chips - step if way == 0 else step
            shard = self.chip_at(ahead) * 2 + self.core
            place = self.slot(shard, self.part(step, way))
            self.copy(place, place, self.ring_sem(step, way), to).wait_recv()
            if step < self.steps:
                passed = self.slot(shard, self.part(step + 1, way))
                self.go(self.copy(passed, passed, self.ring_sem(step + 1, way), to))
            self.go(self.copy(place, place, self.pair_sem(step, way), self.partner))

    def other_own(self):
        shard = self.chip_at(0) * 2 + 1 - self.core
        place = self.slot(shard, None)
        self.copy(place, place, 2 * self.steps, self.partner).wait_recv()

    def other_step(self, step):
        for way in (0, 1):
            ahead = self.chips - step if way == 0 else step
            shard = self.chip_at(ahead) * 2 + 1 - self.core
            place = self.slot(shard, self.part(step, way))
            self.copy(place, place, self.pair_sem(step, way), self.partner).wait_recv()

    def shards(self, step, core):
        far = [self.chip_at(self.chips - step), self.chip_at(step)]
        return [chip * 2 + core for chip in (far if step < self.steps else far[:1])]

    def finish(self):
        if self.local is not None:
            self.keep.wait()
        self.other_own()
        for step in range(1, self.steps + 1):
            self.other_step(step)

    def drain(self):
        for copy in self.sent:
            copy.wait_send()


class LineGather:
    def __init__(self, buffer, part, n_tp, send, recv):
        self.buffer, self.part, self.n_tp, self.send, self.recv = buffer, part, n_tp, send, recv
        self.me = lax.axis_index("tp")

    def copy(self, index, step, way, to):
        return pltpu.make_async_remote_copy(
            src_ref=self.buffer.at[index, self.part],
            dst_ref=self.buffer.at[index, self.part],
            send_sem=self.send.at[2 * (step - 1) + way],
            recv_sem=self.recv.at[2 * (step - 1) + way],
            device_id={"tp": to},
            device_id_type=MESH,
        )

    def launch(self, step):
        me = self.me

        @pl.when((me + 1 < self.n_tp) & (me - step + 1 >= 0))
        def _():
            self.copy(me - step + 1, step, 0, me + 1).start()

        @pl.when((me >= 1) & (me + step - 1 < self.n_tp))
        def _():
            self.copy(me + step - 1, step, 1, me - 1).start()

    def arrive(self, step):
        me = self.me

        @pl.when(me - step >= 0)
        def _():
            self.copy(me - step, step, 0, me).wait_recv()

        @pl.when(me + step < self.n_tp)
        def _():
            self.copy(me + step, step, 1, me).wait_recv()

        if step + 1 < self.n_tp:
            self.launch(step + 1)

    def use(self, step, take):
        me = self.me

        @pl.when(me - step >= 0)
        def _():
            take(me - step)

        @pl.when(me + step < self.n_tp)
        def _():
            take(me + step)

    def drain(self):
        me = self.me
        for step in range(1, self.n_tp):

            @pl.when((me + 1 < self.n_tp) & (me - step + 1 >= 0))
            def _():
                self.copy(me - step + 1, step, 0, me).wait_send()

            @pl.when((me >= 1) & (me + step - 1 < self.n_tp))
            def _():
                self.copy(me + step - 1, step, 1, me).wait_send()


def barrier_with(devices):
    barrier = pltpu.get_barrier_semaphore()
    for device in devices:
        pl.semaphore_signal(barrier, inc=1, device_id=device, device_id_type=MESH)
    pl.semaphore_wait(barrier, len(devices))


CHUNKS = 4


def whole_kernel(
    n_ctx,
    n_tp,
    heads,
    m_local,
    q_ref,
    kv_ref,
    hidden_ref,
    out_ref,
    gain_ref,
    x_proj_ref,
    bc_proj_ref,
    dt_proj_ref,
    bias_ref,
    log_ref,
    skip_ref,
    res_ref,
    y_ref,
    kv_all,
    x_all,
    bc_all,
    dt_all,
    o_all,
    o_full,
    att_all,
    res_all,
    hidden_mine,
    q_rows,
    scores,
    top,
    total,
    mixed,
    sums,
    x_sum,
    bc_sum,
    dt_sum,
    square,
    x_low,
    bc_low,
    mixer_scratch,
    ring_send,
    ring_recv,
    t_send,
    t_recv,
    d_send,
    d_recv,
    a_send,
    a_recv,
    r_send,
    r_recv,
    local,
):
    ctx = lax.axis_index("ctx")
    tp = lax.axis_index("tp")
    tok = q_ref.shape[0]
    half = tok // 2
    head_dim = kv_ref.shape[1] // 2
    cols = hidden_mine.shape[1]
    depth = x_proj_ref.shape[0]
    slab = out_ref.shape[0]
    piece = o_all.shape[1] // n_ctx
    repeat = piece * n_ctx // slab

    def row_gather(index, own, everyone, first, count):
        whole = own.shape[0]

        def slot(i, part):
            start, rows = (0, count) if part is None else (part * (count // 2), count // 2)
            return everyone.at[pl.ds(pl.multiple_of(i * whole + (first + start), rows), rows)]

        return RingGather(
            own.at[pl.ds(first, count)],
            slot,
            n_ctx,
            lambda part: own.at[pl.ds(first + part * (count // 2), count // 2)],
            ring_send.at[index],
            ring_recv.at[index],
            local.at[index],
        )

    kv = row_gather(0, kv_ref, kv_all, 0, tok)
    bc = row_gather(1, bc_proj_ref, bc_all, 0, depth)
    chunk = depth // CHUNKS
    xs = [row_gather(2 + i, x_proj_ref, x_all, i * chunk, chunk) for i in range(CHUNKS)]
    weights = xs + [bc]

    def o_slot(i, part):
        rows = pl.ds(pl.multiple_of(i * piece, piece), piece)
        if part is None:
            return o_all.at[pl.ds(1, n_tp - 1), rows]
        return o_all.at[pl.ds(1, n_tp - 1), rows, pl.ds(part * (cols // 2), cols // 2)]

    o = RingGather(
        o_slot(ctx, None), o_slot, n_ctx, lambda part: o_slot(ctx, part),
        ring_send.at[2 + CHUNKS], ring_recv.at[2 + CHUNKS], None,
    )
    barrier_with(
        [{"ctx": (ctx + ahead) % n_ctx} for ahead in range(1, n_ctx)]
        + [{"tp": (tp + ahead) % n_tp} for ahead in range(1, n_tp)]
    )

    kv.start()
    my_rows = pl.ds(pl.multiple_of((ctx // repeat) * piece, piece), piece)
    my_place = pl.ds(pl.multiple_of(ctx * piece, piece), piece)

    swaps = []
    for ahead in range(1, n_tp):
        to = (tp + ahead) % n_tp
        swap = pltpu.make_async_remote_copy(
            src_ref=out_ref.at[my_rows, pl.ds(pl.multiple_of(to * cols, cols), cols)],
            dst_ref=o_all.at[n_tp - ahead, my_place],
            send_sem=t_send.at[ahead],
            recv_sem=t_recv.at[ahead],
            device_id={"tp": to},
            device_id_type=MESH,
        )
        swap.start()
        swaps.append(swap)
    my_cols = pl.ds(pl.multiple_of(tp * cols, cols), cols)
    keep_o = pltpu.make_async_copy(
        out_ref.at[:, my_cols], o_all.at[0, pl.ds(0, slab)], local.at[2 + CHUNKS]
    )
    keep_o.start()
    get_hidden = pltpu.make_async_copy(
        hidden_ref.at[:, my_cols], hidden_mine, local.at[3 + CHUNKS]
    )
    get_hidden.start()

    for part in range(2):
        for head in range(heads):
            q_rows[part, head * half : (head + 1) * half, :] = q_ref[
                part * half : (part + 1) * half, head * head_dim : (head + 1) * head_dim
            ]
    top[...] = jnp.full_like(top, -1e30)
    total[...] = jnp.zeros_like(total)
    mixed[...] = jnp.zeros_like(mixed)

    scale = 1.0 / math.sqrt(head_dim)
    rows = heads * half
    row_at = lax.broadcasted_iota(jnp.int32, (rows, half), 0) % half
    col_at = lax.broadcasted_iota(jnp.int32, (rows, half), 1)
    causal = col_at <= row_at

    def late_of(shard):
        return (shard - ctx - 1 + n_ctx) // n_ctx

    def block_scores(keys_of, slot, part, start, masked):
        keys = keys_of[pl.ds(pl.multiple_of(start, half), half), :head_dim]
        found = lax.dot_general(
            q_rows[part], keys, (((1,), (1,)), ((), ())), preferred_element_type=F32
        ) * scale
        if masked:
            found = jnp.where(causal, found, -1e30)
        scores[slot] = found
        top[part] = jnp.maximum(top[part], found)

    def shard_scores(shard):
        block_scores(kv_all, shard, 1, shard * tok, False)
        late = late_of(shard)
        block_scores(kv_all, n_ctx + shard, late, shard * tok + late * half, False)

    block_scores(kv_ref, ctx, 1, 0, False)
    block_scores(kv_ref, n_ctx + ctx, 0, 0, True)
    block_scores(kv_ref, 2 * n_ctx, 1, half, True)
    kv.step(1)
    kv.other_own()
    shard_scores(kv.partner)
    for shard in kv.shards(1, kv.core):
        shard_scores(shard)
    for step in range(2, kv.steps + 1):
        kv.step(step)
        if step == 2:
            xs[0].start()
        kv.other_step(step - 1)
        for shard in kv.shards(step - 1, 1 - kv.core) + kv.shards(step, kv.core):
            shard_scores(shard)
    dt_all[ctx] = dt_proj_ref[...]
    dts = []
    for ahead in range(1, n_ctx):
        copy = pltpu.make_async_remote_copy(
            src_ref=dt_proj_ref,
            dst_ref=dt_all.at[ctx],
            send_sem=d_send.at[ahead],
            recv_sem=d_recv.at[ahead],
            device_id={"ctx": (ctx + ahead) % n_ctx},
            device_id_type=MESH,
        )
        copy.start()
        dts.append(copy)
    kv.other_step(kv.steps)
    for shard in kv.shards(kv.steps, 1 - kv.core):
        shard_scores(shard)
    kv.keep.wait()

    for swap in swaps:
        swap.wait_recv()
    o.start()
    for part in range(2):
        top[part] = jnp.broadcast_to(jnp.max(top[part], axis=1, keepdims=True), (rows, half))

    def add_block(slot, part, start):
        found = jnp.exp(scores[slot] - top[part])
        total[part] = total[part] + found
        values = kv_all[pl.ds(pl.multiple_of(start, half), half), head_dim:]
        mixed[part] = mixed[part] + jnp.dot(found.astype(BF16), values, preferred_element_type=F32)

    def early_early(j, carry):
        add_block(n_ctx + j, 0, j * tok)
        return carry

    def late_early(j, carry):
        add_block(j, 1, j * tok)
        return carry

    def late_late(j, carry):
        add_block(n_ctx + j, 1, j * tok + half)
        return carry

    def attend(part):
        ended = (mixed[part] / jnp.sum(total[part], axis=1, keepdims=True)).astype(BF16)
        for head in range(heads):
            att_all[tp, part, :, head * head_dim : (head + 1) * head_dim] = ended[
                head * half : (head + 1) * half
            ]

    attended = [LineGather(att_all, i, n_tp, a_send.at[i], a_recv.at[i]) for i in range(2)]
    lax.fori_loop(0, ctx + 1, early_early, 0)
    attend(0)
    attended[0].launch(1)
    xs[0].step(1)
    xs[1].start()
    lax.fori_loop(0, n_ctx, late_early, 0)
    lax.fori_loop(ctx + 1, n_ctx, late_late, 0)
    add_block(2 * n_ctx, 1, ctx * tok + half)
    attend(1)
    attended[1].launch(1)
    xs[2].start()
    errands = [
        lambda: (o.step(1), xs[3].start()),
        lambda: (xs[1].step(1), o.step(2), bc.start()),
    ]
    errands += [functools.partial(o.step, step) for step in range(3, o.steps + 1)]
    for at, step in enumerate(range(1, n_tp - 1)):
        attended[0].arrive(step)
        attended[1].arrive(step)
        if at < 2:
            errands.pop(0)()
    while errands:
        errands.pop(0)()
    get_hidden.wait()
    keep_o.wait()

    def add_heads(t, part):
        slot = (t - tp + n_tp) % n_tp
        weight = o_full[slot] if repeat > 1 else o_all[slot]
        found = jnp.dot(att_all[t, part], weight, preferred_element_type=F32)
        sums[part] += found.astype(BF16).astype(F32)

    o.finish()
    if repeat > 1:
        o_full[0] = o_all[0, :slab]
        for i in range(slab // piece):
            o_full[1:, i * piece : (i + 1) * piece] = o_all[
                1:, i * repeat * piece : (i * repeat + 1) * piece
            ]
    residual = [LineGather(res_all, i, n_tp, r_send.at[i], r_recv.at[i]) for i in range(2)]
    sums[...] = jnp.zeros_like(sums)
    for part in range(2):
        take = functools.partial(add_heads, part=part)
        take(tp)
        for step in range(1, n_tp - 1):
            attended[part].use(step, take)
        attended[part].arrive(n_tp - 1)
        attended[part].use(n_tp - 1, take)
        at = slice(part * half, (part + 1) * half)
        mine = (hidden_mine[at, :].astype(F32) + sums[part]).astype(BF16)
        res_all[tp, part] = mine
        residual[part].launch(1)
        res_ref[at, :] = mine

    errands = []

    def later(gather, first, last):
        for step in range(first, last + 1):
            errands.append(functools.partial(gather.step, step))

    for gather in xs[:2]:
        later(gather, 2, gather.steps)
    later(xs[2], 1, 1)
    later(xs[3], 1, 1)
    later(xs[2], 2, bc.steps)
    later(bc, 1, 1)
    later(xs[3], 2, bc.steps)
    later(bc, 2, bc.steps)
    share_of = -(-len(errands) // max(1, n_tp - 1))
    x_sum[...] = jnp.zeros_like(x_sum)
    bc_sum[...] = jnp.zeros_like(bc_sum)
    dt_sum[...] = jnp.zeros_like(dt_sum)
    square[...] = jnp.zeros_like(square)
    for step in range(1, n_tp - 1):
        for errand in errands[:share_of]:
            errand()
        errands = errands[share_of:]
        residual[0].arrive(step)
        residual[1].arrive(step)
    for errand in errands:
        errand()
    for ahead, copy in enumerate(dts, 1):
        copy.wait_recv()
    for weight in weights:
        weight.finish()

    def add_features(t):
        part = res_all[t].reshape(tok, cols).astype(F32)
        squares = part * part
        folded = squares[:, :LANES]
        for i in range(1, cols // LANES):
            folded = folded + squares[:, i * LANES : (i + 1) * LANES]
        square[...] += folded
        scaled = (part * gain_ref[t]).astype(BF16)
        at = pl.ds(pl.multiple_of(t * cols, cols), cols)
        x_sum[...] += jnp.dot(scaled, x_all[at, :], preferred_element_type=F32)
        bc_sum[...] += jnp.dot(scaled, bc_all[at, :], preferred_element_type=F32)
        shards = cols // depth
        for i in range(shards):
            dt_sum[...] += lax.dot_general(
                scaled[:, i * depth : (i + 1) * depth], dt_all[t * shards + i],
                (((1,), (1,)), ((), ())), preferred_element_type=F32,
            )

    add_features(tp)
    for step in range(1, n_tp - 1):
        residual[0].use(step, add_features)
    residual[0].arrive(n_tp - 1)
    residual[1].arrive(n_tp - 1)
    residual[0].use(n_tp - 1, add_features)
    mean = jnp.sum(square[...], axis=1, keepdims=True) / (cols * n_tp)
    inverse = lax.rsqrt(mean + 1e-05)
    x_low[...] = (x_sum[...] * inverse).astype(BF16)
    bc_low[...] = (bc_sum[...] * inverse).astype(BF16)
    dt = dt_sum[...] * inverse
    dt = jnp.concatenate([dt, jnp.zeros((tok, LANES - dt.shape[1]), F32)], axis=1)
    mixer(n_ctx, m_local, x_low, bc_low, dt, bias_ref, log_ref, skip_ref, y_ref, *mixer_scratch)

    for gather in [kv, o] + weights:
        gather.drain()
    for copy in swaps + dts:
        copy.wait_send()
    for line in attended + residual:
        line.drain()


def run_kernel(
    n_ctx, n_tp, queries, kv, hidden, out_proj, gain, x_proj, bc_proj, dt_proj, bias, logs, skip,
    m_local,
):
    tok, q_wide = queries.shape
    head_dim = kv.shape[1] // 2
    heads = q_wide // head_dim
    half = tok // 2
    cols = hidden.shape[1] // n_tp
    slab = out_proj.shape[0]
    piece = max(16, slab // n_ctx)
    repeat = piece * n_ctx // slab
    rows = heads * half
    ring = 4 * (n_ctx // 4) + 1
    line = 2 * (n_tp - 1)
    vmem = pl.BlockSpec(memory_space=pltpu.VMEM)
    hbm = pl.BlockSpec(memory_space=pl.ANY)
    depth, wide = x_proj.shape
    bc_wide = bc_proj.shape[1]
    state = bc_wide // 2
    share = wide // n_ctx
    dma = pltpu.SemaphoreType.DMA
    return pl.pallas_call(
        functools.partial(whole_kernel, n_ctx, n_tp, heads, m_local),
        out_shape=(
            jax.ShapeDtypeStruct((tok, cols), BF16),
            jax.ShapeDtypeStruct((tok, wide), BF16),
        ),
        in_specs=[vmem, vmem, hbm, hbm, vmem, hbm, hbm, vmem, vmem, vmem, vmem],
        out_specs=(vmem,) * 2,
        scratch_shapes=[
            pltpu.VMEM((n_ctx * tok, 2 * head_dim), BF16),
            pltpu.VMEM((n_ctx * depth, wide), BF16),
            pltpu.VMEM((n_ctx * depth, bc_wide), BF16),
            pltpu.VMEM((n_ctx,) + dt_proj.shape, BF16),
            pltpu.VMEM((n_tp, n_ctx * piece, cols), BF16),
            pltpu.VMEM((n_tp, slab, cols) if repeat > 1 else (1, 16, LANES), BF16),
            pltpu.VMEM((n_tp, 2, half, q_wide), BF16),
            pltpu.VMEM((n_tp, 2, half, cols), BF16),
            pltpu.VMEM((tok, cols), BF16),
            pltpu.VMEM((2, rows, head_dim), BF16),
            pltpu.VMEM((2 * n_ctx + 1, rows, half), F32),
            pltpu.VMEM((2, rows, half), F32),
            pltpu.VMEM((2, rows, half), F32),
            pltpu.VMEM((2, rows, head_dim), F32),
            pltpu.VMEM((2, half, cols), F32),
            pltpu.VMEM((tok, wide), F32),
            pltpu.VMEM((tok, bc_wide), F32),
            pltpu.VMEM((tok, dt_proj.shape[0]), F32),
            pltpu.VMEM((tok, LANES), F32),
            pltpu.VMEM((tok, wide), BF16),
            pltpu.VMEM((tok, bc_wide), BF16),
            [
                pltpu.VMEM((n_ctx, 2 * share, state), BF16),
                pltpu.VMEM((n_ctx, 2 * share, state), BF16),
                pltpu.VMEM((8, LANES), F32),
                pltpu.VMEM((n_ctx, 8, LANES), F32),
                pltpu.VMEM((n_ctx, 2 * share, state), BF16),
                pltpu.VMEM((n_ctx, 2 * share, state), BF16),
                pltpu.VMEM((wide, state), F32),
                pltpu.VMEM((tok, wide), F32),
                pltpu.VMEM((tok, wide), F32),
            ]
            + [dma((n_ctx,))] * 6,
            dma((3 + CHUNKS, ring)),
            dma((3 + CHUNKS, ring)),
            dma((n_tp,)),
            dma((n_tp,)),
            dma((n_ctx,)),
            dma((n_ctx,)),
            dma((2, line)),
            dma((2, line)),
            dma((2, line)),
            dma((2, line)),
            dma((4 + CHUNKS,)),
        ],
        compiler_params=pltpu.CompilerParams(
            collective_id=0, has_side_effects=True, vmem_limit_bytes=42 * 1024 * 1024
        ),
    )(
        queries, kv, hidden, out_proj, gain.reshape(n_tp, 1, cols), x_proj, bc_proj, dt_proj,
        bias, logs, skip,
    )


def exact_dot(a, b, dims):
    return lax.dot_general(
        a, b, (dims, ((), ())), precision=lax.Precision.HIGHEST, preferred_element_type=F32
    )


def mixer(
    n_ctx,
    m_local,
    x_ref,
    bc_ref,
    dt,
    bias_ref,
    log_ref,
    skip_ref,
    y_ref,
    state_out,
    state_in,
    log_out,
    log_in,
    enter_out,
    enter_in,
    rows_in,
    grown,
    inner,
    s_send,
    s_recv,
    l_send,
    l_recv,
    e_send,
    e_recv,
):
    me = lax.axis_index("ctx")
    tok, wide = x_ref.shape
    half = tok // 2
    state = bc_ref.shape[1] // 2
    head_wide = wide // m_local
    share = wide // n_ctx

    spread = (
        lax.broadcasted_iota(jnp.int32, (LANES, wide), 1) // head_wide
        == lax.broadcasted_iota(jnp.int32, (LANES, wide), 0)
    ).astype(F32).astype(BF16)
    spread = jnp.concatenate([spread, spread], axis=0)

    def widen(values):
        upper = values.astype(BF16)
        lower = (values - upper.astype(F32)).astype(BF16)
        return jnp.dot(
            jnp.concatenate([upper, lower], axis=1), spread, preferred_element_type=F32
        )

    across = lax.broadcasted_iota(jnp.int32, (half, half), 1)
    down = lax.broadcasted_iota(jnp.int32, (half, half), 0)
    causal = across <= down
    lower = causal.astype(F32)

    def padded(ref):
        return jnp.concatenate([ref[...], jnp.zeros((1, LANES - m_local), F32)], axis=1)

    bias, rates = padded(bias_ref), -jnp.exp(padded(log_ref))
    kept = []
    log_out[...] = jnp.zeros_like(log_out)
    for chunk in range(2):
        at = slice(chunk * half, (chunk + 1) * half)
        steps = jax.nn.softplus(dt[at] + bias)
        cumul = exact_dot(lower, steps * rates, ((1,), (0,)))
        last = cumul[half - 1 : half, :]
        log_out[chunk : chunk + 1, :] = last
        tail = widen(jnp.exp(last - cumul) * steps)
        weighted = (x_ref[at, :].astype(F32) * tail).astype(BF16)
        made = lax.dot_general(
            weighted, bc_ref[at, :state], (((0,), (0,)), ((), ())), preferred_element_type=F32
        ).astype(BF16)
        for i in range(n_ctx):
            state_out[i, chunk * share : (chunk + 1) * share, :] = made[i * share : (i + 1) * share]
        kept.append((cumul, steps))

    def transfer(src, dst, send, recv, ahead):
        return pltpu.make_async_remote_copy(
            src_ref=src,
            dst_ref=dst,
            send_sem=send.at[ahead],
            recv_sem=recv.at[ahead],
            device_id={"ctx": (me + ahead) % n_ctx},
            device_id_type=MESH,
        )

    copies = []
    for ahead in range(1, n_ctx):
        to = (me + ahead) % n_ctx
        for copy in (
            transfer(state_out.at[to], state_in.at[me], s_send, s_recv, ahead),
            transfer(log_out, log_in.at[me], l_send, l_recv, ahead),
        ):
            copy.start()
            copies.append(copy)
    state_in[me] = state_out[me]
    log_in[me] = log_out[...]

    skip = widen(jnp.broadcast_to(padded(skip_ref), (16, LANES)))[:1]
    for chunk in range(2):
        at = slice(chunk * half, (chunk + 1) * half)
        cumul, steps = kept[chunk]
        grown[at, :] = widen(jnp.exp(cumul))
        cumul_t, steps_t = cumul.T, steps.T
        gram = lax.dot_general(
            bc_ref[at, state:], bc_ref[at, :state], (((1,), (1,)), ((), ())),
            preferred_element_type=F32,
        )
        gram = jnp.where(causal, gram, 0.0)
        per = LANES // head_wide
        for pair in range(m_local // per):
            lanes = slice(pair * LANES, (pair + 1) * LANES)
            x_pair = x_ref[at, lanes]
            found = None
            for k in range(per):
                head = pair * per + k
                gap = jnp.where(causal, cumul[:, head : head + 1] - cumul_t[head : head + 1, :], 0.0)
                mixing = gram * jnp.exp(gap) * steps_t[head : head + 1, :]
                one = jnp.dot(mixing.astype(BF16), x_pair, preferred_element_type=F32)
                found = one if k == 0 else jnp.where(across // head_wide == k, one, found)
            inner[at, lanes] = found + skip[:, lanes] * x_pair.astype(F32)

    for ahead in range(1, n_ctx):
        src = (me + n_ctx - ahead) % n_ctx
        transfer(state_out.at[src], state_in.at[src], s_send, s_recv, ahead).wait_recv()
        transfer(log_out, log_in.at[src], l_send, l_recv, ahead).wait_recv()

    chosen = (
        (me * share + lax.broadcasted_iota(jnp.int32, (share, LANES), 0)) // head_wide
        == lax.broadcasted_iota(jnp.int32, (share, LANES), 1)
    ).astype(F32)
    running = jnp.zeros((share, state), F32)
    for block in range(2 * n_ctx):
        chunk = block // n_ctx
        src = block if chunk == 0 else 2 * n_ctx - 1 - block
        rows = slice(chunk * share, (chunk + 1) * share)
        enter_out[src, rows, :] = running.astype(BF16)
        logs = jnp.sum(chosen * log_in[src, chunk : chunk + 1, :], axis=1, keepdims=True)
        running = jnp.exp(logs) * running + state_in[src, rows, :].astype(F32)

    for ahead in range(1, n_ctx):
        to = (me + ahead) % n_ctx
        copy = transfer(enter_out.at[to], enter_in.at[me], e_send, e_recv, ahead)
        copy.start()
        copies.append(copy)
    enter_in[me] = enter_out[me]
    for ahead in range(1, n_ctx):
        src = (me + n_ctx - ahead) % n_ctx
        transfer(enter_out.at[src], enter_in.at[src], e_send, e_recv, ahead).wait_recv()
    for chunk in range(2):
        at = slice(chunk * half, (chunk + 1) * half)
        for i in range(n_ctx):
            rows_in[i * share : (i + 1) * share, :] = enter_in[
                i, chunk * share : (chunk + 1) * share, :
            ].astype(F32)
        carried = lax.dot_general(
            bc_ref[at, state:], rows_in[...].astype(BF16), (((1,), (1,)), ((), ())),
            preferred_element_type=F32,
        )
        y_ref[at, :] = (inner[at, :] + grown[at, :] * carried).astype(BF16)
    for copy in copies:
        copy.wait_send()


def body(
    queries,
    key_heads,
    head_values,
    hidden,
    out_proj,
    norm_gain,
    x_proj,
    bc_proj,
    dt_proj,
    dt_bias,
    decay_log,
    skip_gain,
):
    n_ctx = lax.axis_size("ctx")
    n_tp = lax.axis_size("tp")
    tp = lax.axis_index("tp")
    head_dim = key_heads.shape[2]
    q_local = queries.shape[1] // head_dim
    group = q_local * n_tp // key_heads.shape[1]
    m_local = skip_gain.shape[0]
    per_group = m_local * n_tp // bc_proj.shape[1]
    assert q_local <= group and m_local <= per_group
    kv_head = tp * q_local // group
    kv = jnp.concatenate(
        [
            lax.dynamic_index_in_dim(key_heads, kv_head, 1, False),
            lax.dynamic_index_in_dim(head_values, kv_head, 1, False),
        ],
        axis=1,
    )
    bc_mine = lax.dynamic_index_in_dim(bc_proj, tp * m_local // per_group, 1, False)
    rows = -(-m_local // 16) * 16
    dt_mine = jnp.pad(dt_proj.T, ((0, rows - m_local), (0, 0)))
    bias, logs, skip = (part.reshape(1, m_local) for part in (dt_bias, decay_log, skip_gain))
    return run_kernel(
        n_ctx, n_tp, queries, kv, hidden, out_proj, norm_gain, x_proj, bc_mine, dt_mine,
        bias, logs, skip, m_local,
    )


def solution(mesh):
    placed = (
        P("ctx", "tp"),
        P("ctx", None, None),
        P("ctx", None, None),
        P("ctx", None),
        P("tp", None),
        P(),
        P("ctx", "tp"),
        P("ctx", None, None),
        P("ctx", "tp"),
        P("tp"),
        P("tp"),
        P("tp"),
    )
    return jax.shard_map(
        body,
        mesh=mesh,
        in_specs=placed,
        out_specs=(P("ctx", "tp"), P("ctx", "tp")),
        check_vma=False,
    )
```
